256 devices in a mesh: row: 32 (over y, x, core), col: 8 (over z).
Axes of the slice: x: 4, y: 4, z: 8, core: 2. Of those that a mesh axis runs over, the one named last changes fastest.
Arguments:
- points: bfloat16 [32, 98304], P(None, ('row', 'col')), may hold values from -2.6875 to 2.6875
- solution: float32 [4, 98304], P(None, ('row', 'col')), may hold values from -6 to 6
- residual: float32 [4, 98304], P(None, ('row', 'col')), may hold values from -8 to 8
- direction: float32 [4, 98304], P(None, ('row', 'col')), may hold values from -8 to 8
- outscale: float32 [4], replicated, may hold values from 0.5 to 2
- noise_var: float32 [4], replicated, may hold values from 0.05 to 0.5
Outputs:
- solution_new: float32 [4, 98304], P(None, ('row', 'col'))
- residual_new: float32 [4, 98304], P(None, ('row', 'col'))
- direction_new: float32 [4, 98304], P(None, ('row', 'col'))
The draws below stay inside these ranges and needn't reach their ends.
All inputs are finite; a program needn't handle non-finite values.
Results may differ from the reference program's by a relative error of at most 0.0007.
Values may be sent and summed in bfloat16 or wider, within the bound.
No kernel may reach another device: no remote copies, remote signals or barrier semaphores. Data moves between devices by JAX's collectives and lax.ppermute only.
A program may use at most 64 MiB of HBM per device.

```python
import math
import jax
import jax.numpy as jnp
from jax import lax

IN = 32
OBJ = 4
P_SIZE = 384
N = 98304


def draw_residual(key, part):
    key = jax.random.fold_in(key, 11)
    where = jnp.arange(N, dtype=jnp.float32) / N
    base = jnp.clip(jax.random.normal(key, (OBJ, N), jnp.float32), -4.0, 4.0)
    scale = 0.6 + 1.2 * where
    return base * scale[None, :]


def draw_direction(key, part):
    key = jax.random.fold_in(key, 23)
    where = jnp.arange(N, dtype=jnp.float32) / N
    base = jnp.clip(jax.random.normal(key, (OBJ, N), jnp.float32), -4.0, 4.0)
    scale = 0.6 + 1.2 * where
    return base * scale[None, :]


def block_levels(stream_key, dims, cuts, low, largest):
    gain = 1.0
    for dim, parts in cuts:
        steps = jax.random.uniform(jax.random.fold_in(jax.random.fold_in(stream_key, 6), dim), (parts,), jnp.float32, low / len(cuts), largest / len(cuts))
        gain = gain * jnp.repeat(jnp.exp(steps), dims[dim] // parts).reshape((-1,) + (1,) * (len(dims) - 1 - dim))
    return gain


def normal_values(own_key, dims, scale, most, cuts=(), kind=jnp.bfloat16):
    values = jax.random.normal(own_key, dims, jnp.float32) * scale
    if len(cuts) > 0:
        values = block_levels(own_key, dims, cuts, -0.22, 0.18) * values
    return jnp.clip(values, min=-most, max=most).astype(kind)


def setup_inputs(seed: int = 0) -> dict:
    key_list = jax.random.split(jax.random.key(seed), 7)
    return {
        "points": normal_values(key_list[0], (IN, N), 0.45, 2.6875, ((1, 256),)),
        "solution": normal_values(key_list[1], (OBJ, N), 1.0, 6.0, ((1, 256),), jnp.float32),
        "residual": draw_residual(jax.random.fold_in(key_list[6], 71), 0),
        "direction": draw_direction(jax.random.fold_in(key_list[6], 71), 0),
        "outscale": jnp.clip(jnp.exp(jax.random.uniform(key_list[4], (OBJ,), jnp.float32, math.log(0.5), math.log(2.0))), 0.5, 2.0),
        "noise_var": jnp.clip(jnp.exp(jax.random.uniform(key_list[5], (OBJ,), jnp.float32, math.log(0.05), math.log(0.5))), 0.05, 0.5),
    }


def matern(sq_dist):
    scaled = jnp.sqrt(5.0 * jnp.maximum(sq_dist, 0.0))
    return (1.0 + scaled + scaled * scaled / 3.0) * jnp.exp(-scaled)

def squares_of(pts):
    wide = pts.astype(jnp.float32)
    return lax.optimization_barrier(jnp.sum(wide * wide, axis=0))

def kernel_apply(row_pts, row_sq, col_pts, col_sq, col_dir):
    inner = lax.dot_general(row_pts, col_pts, (((0,), (0,)), ((), ())), preferred_element_type=jnp.float32)
    kernel_tile = matern(row_sq[:, None] + col_sq[None, :] - 2.0 * inner)
    return lax.dot_general(col_dir, kernel_tile, (((1,), (1,)), ((), ())), precision=lax.Precision.HIGHEST)

def reference(points, solution, residual, direction, outscale, noise_var):
    sq_norms = squares_of(points)

    def one_block(offset):
        row_pts = lax.dynamic_slice_in_dim(points, offset, P_SIZE, 1)
        row_sq = lax.dynamic_slice_in_dim(sq_norms, offset, P_SIZE, 0)
        return kernel_apply(row_pts, row_sq, points, sq_norms, direction)
    starts = jnp.arange(N // P_SIZE, dtype=jnp.int32) * P_SIZE
    pieces = lax.map(one_block, starts)
    summed = jnp.transpose(pieces, (1, 0, 2)).reshape(OBJ, N)
    image = outscale[:, None] * summed + noise_var[:, None] * direction
    norm_old = lax.optimization_barrier(jnp.sum(residual * residual, axis=1))
    curvature = lax.optimization_barrier(jnp.sum(direction * image, axis=1))
    step_len = norm_old / curvature
    solution_new = solution + step_len[:, None] * direction
    residual_new = residual - step_len[:, None] * image
    norm_new = lax.optimization_barrier(jnp.sum(residual_new * residual_new, axis=1))
    ratio_new = norm_new / (norm_old + 1e-06)
    direction_new = residual_new + ratio_new[:, None] * direction
    return (solution_new, residual_new, direction_new)
```

```python
import functools
import math

import jax
import jax.numpy as jnp
from jax import lax
from jax.experimental import pallas as pl
from jax.experimental.pallas import tpu as pltpu
from jax.sharding import Mesh
from jax.sharding import PartitionSpec as P

SIZES = (4, 4, 2, 8)
AXES = ("y", "x", "core", "z")
GROUP = ("y", "core")
IN, OBJ, WIDTH = 32, 4, 384
BLOCKS = 8
LANES = BLOCKS * WIDTH
HALF = LANES // 2
DEPTH = 128
PACK = 48
LOG2E = 1.0 / math.log(2.0)
X_SCALE = 5.0 * LOG2E * LOG2E
Y_SCALE = 5.0 * LOG2E / 3.0
VMEM = pl.BlockSpec(memory_space=pltpu.VMEM)
SMEM = pl.BlockSpec(memory_space=pltpu.SMEM)


def params():
    return pltpu.CompilerParams(vmem_limit_bytes=48 * 1024 * 1024)


def parts(x, count):
    out = []
    for _ in range(count):
        out.append(x.astype(jnp.bfloat16).astype(jnp.float32))
        x = x - out[-1]
    return out


def rows_of(values, shape):
    where = lax.broadcasted_iota(jnp.int32, shape, 0)
    out = jnp.zeros(shape, jnp.float32)
    for i, value in enumerate(values):
        out = jnp.where(where == i, value, out)
    return out


def row_features(pts, scale, offset, first):
    wide = pts.astype(jnp.float32)
    own = scale * jnp.sum(wide * wide, axis=0, keepdims=True) + offset
    ones = [1.0 if first <= i < first + 3 else 0.0 for i in range(6)]
    extra = rows_of(ones + parts(own, 3), (16, WIDTH))
    zeros = jnp.zeros((16, WIDTH), jnp.float32)
    whole = jnp.concatenate(parts((-2.0 * scale) * wide, 3) + [extra, zeros], axis=0)
    return whole.astype(jnp.bfloat16)


def col_features(pts):
    wide = pts.astype(jnp.float32)
    square = jnp.sum(wide * wide, axis=0, keepdims=True)
    values = parts(X_SCALE * square, 3) + parts(Y_SCALE * square, 3) + [1.0] * 3
    extra = rows_of(values, (16, WIDTH))
    zeros = jnp.zeros((16, WIDTH), jnp.float32)
    whole = jnp.concatenate([wide, wide, wide, extra, zeros], axis=0)
    return whole.T.astype(jnp.bfloat16)


def dot(a, b, dims=((1,), (0,))):
    return lax.dot_general(a, b, (dims, ((), ())), preferred_element_type=jnp.float32)


def entries(bt, ax, ay):
    sq = jnp.maximum(dot(bt, ax), 1e-30)
    a = sq * lax.rsqrt(sq)
    w = (dot(bt, ay) + a) * jnp.exp2(-a)
    hi = w.astype(jnp.bfloat16)
    lo = (w - hi.astype(jnp.float32)).astype(jnp.bfloat16)
    return hi, lo


def row_sums(dc, hi, lo):
    return dot(dc, hi) + dot(dc, lo)


def col_sums(dr, hi, lo):
    nt = ((1,), (1,))
    return dot(dr, hi, nt) + dot(dr, lo, nt)


def pack_kernel(points, direction, out):
    wide = direction[...]
    high, low = parts(wide, 2)
    tail = jnp.concatenate([high, low, jnp.zeros((8, WIDTH), jnp.float32)], axis=0)
    for i in range(BLOCKS):
        out[i, :IN, :] = points[...]
        out[i, IN:, :] = tail.astype(jnp.bfloat16)


def near_kernel(place, rows, cols, ax, ay, dr, row_acc, col_acc, bt):
    h, z = place[0], place[2]
    for i in range(BLOCKS):
        block = rows.at[lax.rem(h + i, BLOCKS)]
        lanes = pl.ds(i * WIDTH, WIDTH)
        pts = block[:IN, :]
        ax[:, lanes] = row_features(pts, X_SCALE, 0.0, 0)
        ay[:, lanes] = row_features(pts, Y_SCALE, LOG2E, 3)
        tail = block[IN:, :]
        dr[:, lanes] = tail
        if i < BLOCKS // 2:
            dr[:, pl.ds(LANES + i * WIDTH, WIDTH)] = jnp.zeros_like(tail) if i == 0 else tail
    row_acc[...] = jnp.zeros_like(row_acc)
    col_acc[...] = jnp.zeros_like(col_acc)

    @pl.loop(0, 5)
    def _(i):
        bt[i] = col_features(cols[lax.rem(z + i, BLOCKS), :IN, :])

    def step(i, at, dr_at):
        here = lax.rem(z + i, BLOCKS)
        lanes = pl.ds(pl.multiple_of(at, WIDTH), HALF)
        hi, lo = entries(bt[i], ax[:, lanes], ay[:, lanes])
        row_acc[:, lanes] += row_sums(cols[here, IN:, :], hi, lo)
        col_acc[here] += col_sums(dr[:, pl.ds(pl.multiple_of(dr_at, WIDTH), HALF)], hi, lo)

    @pl.loop(0, 8)
    def _(s):
        i = jnp.where(s < 6, 1 + s // 2, jnp.where(s == 6, 4, 0))
        tie = jnp.where(z < BLOCKS // 2, 0, WIDTH)
        at = jnp.where(s < 6, lax.rem(s, 2) * HALF, jnp.where(s == 6, tie, 0))
        step(i, at, jnp.where(s == 7, LANES, at))

    lanes = pl.ds(HALF, WIDTH)
    hi, lo = entries(bt[0], ax[:, lanes], ay[:, lanes])
    row_acc[:, lanes] += row_sums(cols[z, IN:, :], hi, lo)


def far_kernel(place, ax, ay, dr, row_in, cols1, cols2, row_out, col1, col2, row_acc, col_acc, bt):
    h, x, z = place[0], place[1], place[2]
    row_acc[...] = row_in[...]
    col_acc[...] = jnp.zeros_like(col_acc)

    def step(cols, base, here, at):
        lanes = pl.ds(pl.multiple_of(at, WIDTH), HALF)
        hi, lo = entries(bt[base + here], ax[:, lanes], ay[:, lanes])
        row_acc[:, lanes] += row_sums(cols[here, IN:, :], hi, lo)
        col_acc[base + here] += col_sums(dr[:, lanes], hi, lo)

    @pl.loop(0, BLOCKS)
    def _(i):
        bt[i] = col_features(cols1[i, :IN, :])
        bt[BLOCKS + i] = col_features(cols2[i, :IN, :])

    @pl.loop(0, 2 * BLOCKS)
    def _(s):
        step(cols1, 0, s // 2, lax.rem(s, 2) * HALF)

    shift = jnp.where(x < 2, 0, 1)

    @pl.loop(0, BLOCKS)
    def _(s):
        step(cols2, BLOCKS, lax.rem(z + shift + s // 2, BLOCKS), lax.rem(s, 2) * HALF)

    for i in range(BLOCKS):
        got = row_acc[:, pl.ds(i * WIDTH, WIDTH)]
        row_out[lax.rem(h + i, BLOCKS)] = got[:OBJ] + got[OBJ : 2 * OBJ]
        col1[i] = col_acc[i, :OBJ, :] + col_acc[i, OBJ : 2 * OBJ, :]
        col2[i] = col_acc[BLOCKS + i, :OBJ, :] + col_acc[BLOCKS + i, OBJ : 2 * OBJ, :]


def join_kernel(near, one, two, out):
    for i in range(BLOCKS):
        out[i] = near[i, :OBJ, :] + near[i, OBJ : 2 * OBJ, :] + one[i] + two[i]


def image_kernel(by_rows, by_cols, direction, residual, outscale, noise, image, sums):
    total = jnp.zeros((OBJ, WIDTH), jnp.float32)
    for i in range(BLOCKS):
        total = total + by_rows[i] + by_cols[i]
    d, r = direction[...], residual[...]
    got = outscale[...] * (total * math.log(2.0)) + noise[...] * d
    image[...] = got
    lane = lax.broadcasted_iota(jnp.int32, (OBJ, 128), 1)
    row = jnp.zeros((OBJ, 128), jnp.float32)
    for i, product in enumerate((r * r, d * got, r * got, got * got)):
        row = jnp.where(lane == i, jnp.sum(product, axis=1, keepdims=True), row)
    for i in range(sums.shape[0]):
        sums[i] = row


def update_kernel(sums, solution, residual, direction, image, solution_new, residual_new, direction_new):
    total = jnp.sum(sums[...], axis=0)
    norm_old, curvature = total[:, 0:1], total[:, 1:2]
    cross, square = total[:, 2:3], total[:, 3:4]
    step_len = norm_old / curvature
    norm_new = jnp.maximum(norm_old - 2.0 * step_len * cross + step_len * step_len * square, 0.0)
    ratio_new = norm_new / (norm_old + 1e-06)
    d = direction[...]
    solution_new[...] = solution[...] + step_len * d
    moved = residual[...] - step_len * image[...]
    residual_new[...] = moved
    direction_new[...] = moved + ratio_new * d


def f32(*shape):
    return jax.ShapeDtypeStruct(shape, jnp.float32)


def bf16(*shape):
    return jax.ShapeDtypeStruct(shape, jnp.bfloat16)


def exchanged(x, axis):
    return lax.all_to_all(x, axis, 0, 0)


def from_ahead(x, by):
    length = lax.axis_size("x")
    return lax.ppermute(x, "x", [(i, (i - by) % length) for i in range(length)])


def shards(points, solution, residual, direction, outscale, noise_var):
    place = jnp.stack([lax.axis_index(GROUP), lax.axis_index("x"), lax.axis_index("z")])
    place = place.astype(jnp.int32)
    packed = pl.pallas_call(
        pack_kernel,
        in_specs=[VMEM] * 2,
        out_specs=VMEM,
        out_shape=bf16(BLOCKS, PACK, WIDTH),
    )(points, direction)
    cols = exchanged(packed, "z")
    cols1, cols2 = from_ahead(cols, 1), from_ahead(cols, 2)
    rows = exchanged(packed, GROUP)
    ax, ay, dr, row_acc, col_near = pl.pallas_call(
        near_kernel,
        in_specs=[SMEM, VMEM, VMEM],
        out_specs=[VMEM] * 5,
        out_shape=[
            bf16(DEPTH, LANES),
            bf16(DEPTH, LANES),
            bf16(16, LANES + HALF),
            f32(16, LANES),
            f32(BLOCKS, 16, WIDTH),
        ],
        scratch_shapes=[pltpu.VMEM((5, WIDTH, DEPTH), jnp.bfloat16)],
        compiler_params=params(),
        cost_estimate=pl.CostEstimate(flops=8 * 10**9, bytes_accessed=10**6, transcendentals=10**7),
    )(place, rows, cols)
    by_rows, col1, col2 = pl.pallas_call(
        far_kernel,
        in_specs=[SMEM] + [VMEM] * 6,
        out_specs=[VMEM] * 3,
        out_shape=[f32(BLOCKS, OBJ, WIDTH)] * 3,
        scratch_shapes=[
            pltpu.VMEM((16, LANES), jnp.float32),
            pltpu.VMEM((2 * BLOCKS, 16, WIDTH), jnp.float32),
            pltpu.VMEM((2 * BLOCKS, WIDTH, DEPTH), jnp.bfloat16),
        ],
        compiler_params=params(),
        cost_estimate=pl.CostEstimate(flops=24 * 10**9, bytes_accessed=10**6, transcendentals=10**7),
    )(place, ax, ay, dr, row_acc, cols1, cols2)
    col1, col2 = from_ahead(col1, -1), from_ahead(col2, -2)
    by_rows = exchanged(by_rows, GROUP)
    by_cols = pl.pallas_call(
        join_kernel,
        in_specs=[VMEM] * 3,
        out_specs=VMEM,
        out_shape=f32(BLOCKS, OBJ, WIDTH),
    )(col_near, col1, col2)
    by_cols = exchanged(by_cols, "z")
    image, sums = pl.pallas_call(
        image_kernel,
        in_specs=[VMEM] * 6,
        out_specs=[VMEM] * 2,
        out_shape=[f32(OBJ, WIDTH), f32(math.prod(SIZES), OBJ, 128)],
    )(by_rows, by_cols, direction, residual, outscale[:, None], noise_var[:, None])
    sums = exchanged(sums, AXES)
    return pl.pallas_call(
        update_kernel,
        in_specs=[VMEM] * 5,
        out_specs=[VMEM] * 3,
        out_shape=[f32(OBJ, WIDTH)] * 3,
    )(sums, solution, residual, direction, image)


def solution(mesh):
    own = Mesh(mesh.devices.reshape(SIZES), AXES)
    split = P(None, AXES)
    return jax.shard_map(
        shards,
        mesh=own,
        in_specs=(split, split, split, split, P(), P()),
        out_specs=(split, split, split),
        check_vma=False,
    )
```

```python
import functools
import math

import jax
import jax.numpy as jnp
from jax import lax
from jax.experimental import pallas as pl
from jax.experimental.pallas import tpu as pltpu
from jax.sharding import Mesh
from jax.sharding import PartitionSpec as P

SIZES = (4, 4, 2, 8)
AXES = ("y", "x", "core", "z")
GROUP = ("y", "core")
IN, OBJ, WIDTH = 32, 4, 384
BLOCKS = 8
LANES = BLOCKS * WIDTH
HALF = LANES // 2
DEPTH = 128
PACK = 48
LOG2E = 1.0 / math.log(2.0)
SCALE = 5.0 / 9.0
VMEM = pl.BlockSpec(memory_space=pltpu.VMEM)
SMEM = pl.BlockSpec(memory_space=pltpu.SMEM)


def params():
    return pltpu.CompilerParams(vmem_limit_bytes=48 * 1024 * 1024)


def parts(x, count):
    out = []
    for _ in range(count):
        out.append(x.astype(jnp.bfloat16).astype(jnp.float32))
        x = x - out[-1]
    return out


def rows_of(values, shape):
    where = lax.broadcasted_iota(jnp.int32, shape, 0)
    out = jnp.zeros(shape, jnp.float32)
    for i, value in enumerate(values):
        out = jnp.where(where == i, value, out)
    return out


def row_features(pts):
    wide = pts.astype(jnp.float32)
    own = SCALE * jnp.sum(wide * wide, axis=0, keepdims=True)
    extra = rows_of([1.0] * 3 + parts(own, 3), (16, WIDTH))
    zeros = jnp.zeros((16, WIDTH), jnp.float32)
    whole = jnp.concatenate(parts((-2.0 * SCALE) * wide, 3) + [extra, zeros], axis=0)
    return whole.astype(jnp.bfloat16)


def col_features(pts):
    wide = pts.astype(jnp.float32)
    own = SCALE * jnp.sum(wide * wide, axis=0, keepdims=True)
    extra = rows_of(parts(own, 3) + [1.0] * 3, (16, WIDTH))
    zeros = jnp.zeros((16, WIDTH), jnp.float32)
    whole = jnp.concatenate([wide, wide, wide, extra, zeros], axis=0)
    return whole.T.astype(jnp.bfloat16)


def dot(a, b, dims=((1,), (0,))):
    return lax.dot_general(a, b, (dims, ((), ())), preferred_element_type=jnp.float32)


def weights(sq):
    sq = jnp.maximum(sq, 1e-30)
    v = sq * lax.rsqrt(sq)
    w = ((sq + v) + 1.0 / 3.0) * jnp.exp2(v * (-3.0 * LOG2E))
    hi = w.astype(jnp.bfloat16)
    lo = (w - hi.astype(jnp.float32)).astype(jnp.bfloat16)
    return hi, lo


def both(a, hi, lo, dims=((1,), (0,))):
    return dot(a, hi, dims) + dot(a, lo, dims)


TRANSPOSED = ((1,), (1,))
STRIP = 256


def pipeline(count, place_of, bt, ax, dr, dc, row_acc, col_acc, stages):
    xa, xb, ha, hb, la, lb = stages
    hb[...] = jnp.zeros_like(hb)
    lb[...] = jnp.zeros_like(lb)

    def distances(step, out, o):
        i, at, _ = place_of(step)
        out[:, o : o + STRIP] = dot(bt[i], ax[:, pl.ds(pl.multiple_of(at + o, 128), STRIP)])

    def by_col(step, hi, lo, o):
        _, _, at = place_of(step)
        lanes = pl.ds(pl.multiple_of(at + o, 128), STRIP)
        return both(dr[:, lanes], hi[:, o : o + STRIP], lo[:, o : o + STRIP], TRANSPOSED)

    def by_row(step, hi, lo, o):
        i, at, _ = place_of(step)
        lanes = pl.ds(pl.multiple_of(at + o, 128), STRIP)
        row_acc[:, lanes] += both(dc[i], hi[:, o : o + STRIP], lo[:, o : o + STRIP])

    def half(step, x, x_next, hi, lo, hi_last, lo_last):
        last, following = jnp.maximum(step - 1, 0), jnp.minimum(step + 1, count - 1)
        total = None
        for o in range(0, HALF, STRIP):
            distances(following, x_next, o)
            part = by_col(last, hi_last, lo_last, o)
            total = part if total is None else total + part
            by_row(last, hi_last, lo_last, o)
            got = weights(x[:, o : o + STRIP])
            hi[:, o : o + STRIP], lo[:, o : o + STRIP] = got
        col_acc[place_of(last)[0]] += total

    for o in range(0, HALF, STRIP):
        distances(0, xa, o)

    @pl.loop(0, count // 2)
    def _(pair):
        half(2 * pair, xa, xb, ha, la, hb, lb)
        half(2 * pair + 1, xb, xa, hb, lb, ha, la)

    total = None
    for o in range(0, HALF, STRIP):
        part = by_col(count - 1, hb, lb, o)
        total = part if total is None else total + part
        by_row(count - 1, hb, lb, o)
    col_acc[place_of(count - 1)[0]] += total


def stages():
    block = (WIDTH, HALF)
    return [pltpu.VMEM(block, jnp.float32)] * 2 + [pltpu.VMEM(block, jnp.bfloat16)] * 4


def folded(x):
    return x[:OBJ] + x[OBJ : 2 * OBJ]


def pack_kernel(points, direction, residual, solution, out, own, kept):
    wide = direction[...]
    high, low = parts(wide, 2)
    tail = jnp.concatenate([high, low, jnp.zeros((8, WIDTH), jnp.float32)], axis=0)
    tail = tail.astype(jnp.bfloat16)
    own[0, :IN, :] = points[...]
    own[0, IN:, :] = tail
    for i in range(BLOCKS):
        out[i, :IN, :] = points[...]
        out[i, IN:, :] = tail
    kept[0] = wide
    kept[1] = residual[...]
    kept[2] = solution[...]


def near_kernel(place, r0, r1, r2, r3, cols, ax, dr, row_acc, col_near, rows, bt, dc, col_acc, *work):
    y, core, z = place[0], place[1], place[3]
    h = 2 * y + core
    for k, ref in enumerate((r0, r1, r2, r3)):
        rows[2 * k] = ref[0]
        rows[2 * k + 1] = ref[1]
    for i in range(BLOCKS):
        there = lax.rem(h + i, BLOCKS)
        away = lax.rem(y - there // 2 + 4, 4)
        other = jnp.where(lax.rem(there, 2) == core, 0, 1)
        block = rows[2 * away + other]
        lanes = pl.ds(i * WIDTH, WIDTH)
        ax[:, lanes] = row_features(block[:IN])
        tail = block[IN:]
        dr[:, lanes] = tail
        if i < BLOCKS // 2:
            dr[:, pl.ds(LANES + i * WIDTH, WIDTH)] = jnp.zeros_like(tail) if i == 0 else tail
    row_acc[...] = jnp.zeros_like(row_acc)
    col_acc[...] = jnp.zeros_like(col_acc)
    for i in range(5):
        block = cols[lax.rem(z + i, BLOCKS)]
        bt[i] = col_features(block[:IN])
        dc[i] = block[IN:]
    tie = jnp.where(z < BLOCKS // 2, 0, WIDTH)

    def place_of(s):
        i = jnp.where(s < 6, 1 + s // 2, jnp.where(s == 6, 4, 0))
        at = jnp.where(s < 6, lax.rem(s, 2) * HALF, jnp.where(s == 6, tie, 0))
        return i, at, jnp.where(s == 7, LANES, at)

    pipeline(8, place_of, bt, ax, dr, dc, row_acc, col_acc, work)

    lanes = pl.ds(HALF, WIDTH)
    hi, lo = weights(dot(bt[0], ax[:, lanes]))
    row_acc[:, lanes] += both(dc[0], hi, lo)
    for i in range(BLOCKS):
        got = folded(col_acc[i]) if i < 5 else jnp.zeros((OBJ, WIDTH), jnp.float32)
        col_near[lax.rem(z + i, BLOCKS)] = got


def far_kernel(place, ax, dr, row_in, cols1, cols2, row_out, col1, col2, row_acc, bt, dc, col_acc, *work):
    y, core, x, z = place[0], place[1], place[2], place[3]
    h = 2 * y + core
    row_acc[...] = row_in[...]
    col_acc[...] = jnp.zeros_like(col_acc)
    first = z + jnp.where(x < 2, 0, 1)
    for i in range(12):
        block = cols1[i] if i < BLOCKS else cols2[lax.rem(first + i, BLOCKS)]
        bt[i] = col_features(block[:IN])
        dc[i] = block[IN:]

    def place_of(s):
        at = lax.rem(s, 2) * HALF
        return s // 2, at, at

    pipeline(24, place_of, bt, ax, dr, dc, row_acc, col_acc, work)
    for i in range(BLOCKS):
        row_out[lax.rem(h + i, BLOCKS)] = folded(row_acc[:, pl.ds(i * WIDTH, WIDTH)])
        col1[i] = folded(col_acc[i])
        got = folded(col_acc[BLOCKS + i]) if i < 4 else jnp.zeros((OBJ, WIDTH), jnp.float32)
        col2[lax.rem(first + i, BLOCKS)] = got


def join_kernel(near, one, two, out):
    out[...] = near[...] + one[...] + two[...]


def image_kernel(by_rows, by_cols, kept, outscale, noise, image, sums):
    total = jnp.zeros((OBJ, WIDTH), jnp.float32)
    for i in range(BLOCKS):
        total = total + by_rows[i] + by_cols[i]
    d, r = kept[0], kept[1]
    objective = lax.broadcasted_iota(jnp.int32, (OBJ, 1), 0)
    scale, noisy = jnp.zeros((OBJ, 1), jnp.float32), jnp.zeros((OBJ, 1), jnp.float32)
    for o in range(OBJ):
        scale = jnp.where(objective == o, outscale[o], scale)
        noisy = jnp.where(objective == o, noise[o], noisy)
    got = scale * (3.0 * total) + noisy * d
    image[...] = got
    products = jnp.concatenate([r * r, d * got, r * got, got * got], axis=0)
    column = jnp.sum(products, axis=1, keepdims=True)
    shape = (4 * OBJ, 128)
    diagonal = lax.broadcasted_iota(jnp.int32, shape, 0) == lax.broadcasted_iota(jnp.int32, shape, 1)
    row = jnp.sum(jnp.where(diagonal, column, 0.0), axis=0, keepdims=True)
    sums[...] = jnp.broadcast_to(row, sums.shape)


def update_kernel(sums, kept, image, solution_new, residual_new, direction_new):
    total = jnp.sum(sums[...], axis=0, keepdims=True)
    lane = lax.broadcasted_iota(jnp.int32, (OBJ, 128), 1) - lax.broadcasted_iota(jnp.int32, (OBJ, 128), 0)

    def kind(k):
        return jnp.sum(jnp.where(lane == k * OBJ, total, 0.0), axis=1, keepdims=True)

    norm_old, curvature, cross, square = kind(0), kind(1), kind(2), kind(3)
    step_len = norm_old / curvature
    norm_new = jnp.maximum(norm_old - 2.0 * step_len * cross + step_len * step_len * square, 0.0)
    ratio_new = norm_new / (norm_old + 1e-06)
    d = kept[0]
    solution_new[...] = kept[2] + step_len * d
    moved = kept[1] - step_len * image[...]
    residual_new[...] = moved
    direction_new[...] = moved + ratio_new * d


def f32(*shape):
    return jax.ShapeDtypeStruct(shape, jnp.float32)


def bf16(*shape):
    return jax.ShapeDtypeStruct(shape, jnp.bfloat16)


def exchanged(x, axis):
    return lax.all_to_all(x, axis, 0, 0)


def from_ahead(x, axis, by):
    length = lax.axis_size(axis)
    return lax.ppermute(x, axis, [(i, (i - by) % length) for i in range(length)])


def shards(points, solution, residual, direction, outscale, noise_var):
    devices = math.prod(SIZES)
    place = jnp.stack([lax.axis_index(a) for a in ("y", "core", "x", "z")]).astype(jnp.int32)
    packed, own, kept = pl.pallas_call(
        pack_kernel,
        in_specs=[VMEM] * 4,
        out_specs=[VMEM] * 3,
        out_shape=[bf16(BLOCKS, PACK, WIDTH), bf16(1, PACK, WIDTH), f32(3, OBJ, WIDTH)],
    )(points, direction, residual, solution)
    pair = jnp.concatenate([own, from_ahead(own, "core", 1)], axis=0)
    rows = [pair] + [from_ahead(pair, "y", -k) for k in (1, 2, 3)]
    cols = exchanged(packed, "z")
    cols1, cols2 = from_ahead(cols, "x", 1), from_ahead(cols, "x", 2)
    ax, dr, row_acc, col_near = pl.pallas_call(
        near_kernel,
        in_specs=[SMEM] + [VMEM] * 5,
        out_specs=[VMEM] * 4,
        out_shape=[
            bf16(DEPTH, LANES),
            bf16(16, LANES + HALF),
            f32(16, LANES),
            f32(BLOCKS, OBJ, WIDTH),
        ],
        scratch_shapes=[
            pltpu.VMEM((BLOCKS, PACK, WIDTH), jnp.bfloat16),
            pltpu.VMEM((5, WIDTH, DEPTH), jnp.bfloat16),
            pltpu.VMEM((5, 16, WIDTH), jnp.bfloat16),
            pltpu.VMEM((5, 16, WIDTH), jnp.float32),
        ]
        + stages(),
        compiler_params=params(),
        cost_estimate=pl.CostEstimate(flops=8 * 10**9, bytes_accessed=10**6, transcendentals=10**7),
    )(place, *rows, cols)
    by_rows, col1, col2 = pl.pallas_call(
        far_kernel,
        in_specs=[SMEM] + [VMEM] * 5,
        out_specs=[VMEM] * 3,
        out_shape=[f32(BLOCKS, OBJ, WIDTH)] * 3,
        scratch_shapes=[
            pltpu.VMEM((16, LANES), jnp.float32),
            pltpu.VMEM((12, WIDTH, DEPTH), jnp.bfloat16),
            pltpu.VMEM((12, 16, WIDTH), jnp.bfloat16),
            pltpu.VMEM((12, 16, WIDTH), jnp.float32),
        ]
        + stages(),
        compiler_params=params(),
        cost_estimate=pl.CostEstimate(flops=24 * 10**9, bytes_accessed=10**6, transcendentals=10**7),
    )(place, ax, dr, row_acc, cols1, cols2)
    col1, col2 = from_ahead(col1, "x", -1), from_ahead(col2, "x", -2)
    by_rows = exchanged(by_rows, GROUP)
    by_cols = pl.pallas_call(
        join_kernel,
        in_specs=[VMEM] * 3,
        out_specs=VMEM,
        out_shape=f32(BLOCKS, OBJ, WIDTH),
    )(col_near, col1, col2)
    by_cols = exchanged(by_cols, "z")
    image, sums = pl.pallas_call(
        image_kernel,
        in_specs=[VMEM] * 3 + [SMEM] * 2,
        out_specs=[VMEM] * 2,
        out_shape=[f32(OBJ, WIDTH), f32(devices, 128)],
    )(by_rows, by_cols, kept, outscale, noise_var)
    sums = exchanged(sums.reshape(devices, 1, 128), AXES).reshape(devices, 128)
    return pl.pallas_call(
        update_kernel,
        in_specs=[VMEM] * 3,
        out_specs=[VMEM] * 3,
        out_shape=[f32(OBJ, WIDTH)] * 3,
    )(sums, kept, image)


def solution(mesh):
    own = Mesh(mesh.devices.reshape(SIZES), AXES)
    split = P(None, AXES)
    return jax.shard_map(
        shards,
        mesh=own,
        in_specs=(split, split, split, split, P(), P()),
        out_specs=(split, split, split),
        check_vma=False,
    )
```

```python
import functools
import math

import jax
import jax.numpy as jnp
from jax import lax
from jax.experimental import pallas as pl
from jax.experimental.pallas import tpu as pltpu
from jax.sharding import Mesh
from jax.sharding import PartitionSpec as P

SIZES = (4, 4, 2, 8)
AXES = ("y", "x", "core", "z")
GROUP = ("y", "core")
IN, OBJ, WIDTH = 32, 4, 384
BLOCKS = 8
LANES = BLOCKS * WIDTH
HALF = LANES // 2
DEPTH = 128
PACK = 48
LOG2E = 1.0 / math.log(2.0)
SCALE = 5.0 / 9.0
VMEM = pl.BlockSpec(memory_space=pltpu.VMEM)
SMEM = pl.BlockSpec(memory_space=pltpu.SMEM)


def params(mebibytes=48):
    return pltpu.CompilerParams(vmem_limit_bytes=mebibytes * 1024 * 1024)


def parts(x, count):
    out = []
    for _ in range(count):
        out.append(x.astype(jnp.bfloat16).astype(jnp.float32))
        x = x - out[-1]
    return out


def rows_of(values, shape):
    where = lax.broadcasted_iota(jnp.int32, shape, 0)
    out = jnp.zeros(shape, jnp.float32)
    for i, value in enumerate(values):
        out = jnp.where(where == i, value, out)
    return out


def row_features(pts):
    wide = pts.astype(jnp.float32)
    own = SCALE * jnp.sum(wide * wide, axis=0, keepdims=True)
    extra = rows_of([1.0] * 3 + parts(own, 3), (16, WIDTH))
    zeros = jnp.zeros((16, WIDTH), jnp.float32)
    whole = jnp.concatenate(parts((-2.0 * SCALE) * wide, 3) + [extra, zeros], axis=0)
    return whole.astype(jnp.bfloat16)


def col_features(pts):
    wide = pts.astype(jnp.float32)
    own = SCALE * jnp.sum(wide * wide, axis=0, keepdims=True)
    extra = rows_of(parts(own, 3) + [1.0] * 3, (16, WIDTH))
    zeros = jnp.zeros((16, WIDTH), jnp.float32)
    whole = jnp.concatenate([wide, wide, wide, extra, zeros], axis=0)
    return whole.T.astype(jnp.bfloat16)


def dot(a, b, dims=((1,), (0,))):
    return lax.dot_general(a, b, (dims, ((), ())), preferred_element_type=jnp.float32)


def weights(sq):
    sq = jnp.maximum(sq, 1e-30)
    v = sq * lax.rsqrt(sq)
    w = ((sq + v) + 1.0 / 3.0) * jnp.exp2(v * (-3.0 * LOG2E))
    hi = w.astype(jnp.bfloat16)
    lo = (w - hi.astype(jnp.float32)).astype(jnp.bfloat16)
    return hi, lo


def both(a, hi, lo, dims=((1,), (0,))):
    return dot(a, hi, dims) + dot(a, lo, dims)


TRANSPOSED = ((1,), (1,))
STRIP = 256


def pipeline(count, place_of, bt, ax, dr, dc, row_acc, col_acc, stages):
    xa, xb, ha, hb, la, lb = stages
    hb[...] = jnp.zeros_like(hb)
    lb[...] = jnp.zeros_like(lb)

    def distances(step, out, o):
        i, at, _ = place_of(step)
        out[:, o : o + STRIP] = dot(bt[i], ax[:, pl.ds(pl.multiple_of(at + o, 128), STRIP)])

    def by_col(step, hi, lo, o):
        _, _, at = place_of(step)
        lanes = pl.ds(pl.multiple_of(at + o, 128), STRIP)
        return both(dr[:, lanes], hi[:, o : o + STRIP], lo[:, o : o + STRIP], TRANSPOSED)

    def by_row(step, hi, lo, o):
        i, at, _ = place_of(step)
        lanes = pl.ds(pl.multiple_of(at + o, 128), STRIP)
        row_acc[:, lanes] += both(dc[i], hi[:, o : o + STRIP], lo[:, o : o + STRIP])

    def half(step, x, x_next, hi, lo, hi_last, lo_last):
        last, following = jnp.maximum(step - 1, 0), jnp.minimum(step + 1, count - 1)
        total = None
        for o in range(0, HALF, STRIP):
            distances(following, x_next, o)
            part = by_col(last, hi_last, lo_last, o)
            total = part if total is None else total + part
            by_row(last, hi_last, lo_last, o)
            got = weights(x[:, o : o + STRIP])
            hi[:, o : o + STRIP], lo[:, o : o + STRIP] = got
        col_acc[place_of(last)[0]] += total

    for o in range(0, HALF, STRIP):
        distances(0, xa, o)

    @pl.loop(0, count // 2)
    def _(pair):
        half(2 * pair, xa, xb, ha, la, hb, lb)
        half(2 * pair + 1, xb, xa, hb, lb, ha, la)

    total = None
    for o in range(0, HALF, STRIP):
        part = by_col(count - 1, hb, lb, o)
        total = part if total is None else total + part
        by_row(count - 1, hb, lb, o)
    col_acc[place_of(count - 1)[0]] += total


def stages():
    block = (WIDTH, HALF)
    return [pltpu.VMEM(block, jnp.float32)] * 2 + [pltpu.VMEM(block, jnp.bfloat16)] * 4


def folded(x):
    return x[:OBJ] + x[OBJ : 2 * OBJ]


def pack_kernel(points, direction, residual, solution, outscale, noise, out, own, kept):
    wide = direction[...]
    high, low = parts(wide, 2)
    tail = jnp.concatenate([high, low, jnp.zeros((8, WIDTH), jnp.float32)], axis=0)
    tail = tail.astype(jnp.bfloat16)
    own[0, :IN, :] = points[...]
    own[0, IN:, :] = tail
    for i in range(BLOCKS):
        out[i, :IN, :] = points[...]
        out[i, IN:, :] = tail
    kept[0] = wide
    kept[1] = residual[...]
    kept[2] = solution[...]
    for o in range(OBJ):
        kept[3, o : o + 1, :] = jnp.full((1, WIDTH), 3.0 * outscale[o], jnp.float32)
        kept[4, o : o + 1, :] = jnp.full((1, WIDTH), noise[o], jnp.float32)


def near_kernel(place, r0, r1, r2, r3, cols, ax, dr, row_acc, col_near, rows, bt, dc, col_acc, *work):
    y, core, z = place[0], place[1], place[3]
    h = 2 * y + core
    for k, ref in enumerate((r0, r1, r2, r3)):
        rows[2 * k] = ref[0]
        rows[2 * k + 1] = ref[1]
    for i in range(BLOCKS):
        there = lax.rem(h + i, BLOCKS)
        away = lax.rem(y - there // 2 + 4, 4)
        other = jnp.where(lax.rem(there, 2) == core, 0, 1)
        block = rows[2 * away + other]
        lanes = pl.ds(i * WIDTH, WIDTH)
        ax[:, lanes] = row_features(block[:IN])
        tail = block[IN:]
        dr[:, lanes] = tail
        if i < BLOCKS // 2:
            dr[:, pl.ds(LANES + i * WIDTH, WIDTH)] = jnp.zeros_like(tail) if i == 0 else tail
    row_acc[...] = jnp.zeros_like(row_acc)
    col_acc[...] = jnp.zeros_like(col_acc)
    for i in range(5):
        block = cols[lax.rem(z + i, BLOCKS)]
        bt[i] = col_features(block[:IN])
        dc[i] = block[IN:]
    tie = jnp.where(z < BLOCKS // 2, 0, WIDTH)

    def place_of(s):
        i = jnp.where(s < 6, 1 + s // 2, jnp.where(s == 6, 4, 0))
        at = jnp.where(s < 6, lax.rem(s, 2) * HALF, jnp.where(s == 6, tie, 0))
        return i, at, jnp.where(s == 7, LANES, at)

    pipeline(8, place_of, bt, ax, dr, dc, row_acc, col_acc, work)

    lanes = pl.ds(HALF, WIDTH)
    hi, lo = weights(dot(bt[0], ax[:, lanes]))
    row_acc[:, lanes] += both(dc[0], hi, lo)
    for i in range(BLOCKS):
        got = folded(col_acc[i]) if i < 5 else jnp.zeros((OBJ, WIDTH), jnp.float32)
        col_near[lax.rem(z + i, BLOCKS)] = got


def far_kernel(place, ax, dr, row_in, cols1, cols2, row_out, col1, col2, row_acc, bt, dc, col_acc, *work):
    y, core, x, z = place[0], place[1], place[2], place[3]
    h = 2 * y + core
    row_acc[...] = row_in[...]
    col_acc[...] = jnp.zeros_like(col_acc)
    first = z + jnp.where(x < 2, 0, 1)
    for i in range(12):
        block = cols1[i] if i < BLOCKS else cols2[lax.rem(first + i, BLOCKS)]
        bt[i] = col_features(block[:IN])
        dc[i] = block[IN:]

    def place_of(s):
        at = lax.rem(s, 2) * HALF
        return s // 2, at, at

    pipeline(24, place_of, bt, ax, dr, dc, row_acc, col_acc, work)
    for i in range(BLOCKS):
        row_out[lax.rem(h + i, BLOCKS)] = folded(row_acc[:, pl.ds(i * WIDTH, WIDTH)])
        col1[i] = folded(col_acc[i])
        got = folded(col_acc[BLOCKS + i]) if i < 4 else jnp.zeros((OBJ, WIDTH), jnp.float32)
        col2[lax.rem(first + i, BLOCKS)] = got


def join_kernel(near, one, two, out):
    out[...] = near[...] + one[...] + two[...]


def image_kernel(by_rows, by_cols, kept, image, sums):
    total = jnp.zeros((OBJ, WIDTH), jnp.float32)
    for i in range(BLOCKS):
        total = total + by_rows[i] + by_cols[i]
    d, r = kept[0], kept[1]
    got = kept[3] * total + kept[4] * d
    image[...] = got
    products = jnp.concatenate([r * r, d * got, r * got, got * got], axis=0)
    column = jnp.sum(products, axis=1, keepdims=True)
    shape = (4 * OBJ, 128)
    diagonal = lax.broadcasted_iota(jnp.int32, shape, 0) == lax.broadcasted_iota(jnp.int32, shape, 1)
    row = jnp.sum(jnp.where(diagonal, column, 0.0), axis=0, keepdims=True)
    sums[...] = jnp.broadcast_to(row, sums.shape)


def update_kernel(sums, kept, image, solution_new, residual_new, direction_new):
    total = jnp.sum(sums[...], axis=0, keepdims=True)
    lane = lax.broadcasted_iota(jnp.int32, (OBJ, 128), 1) - lax.broadcasted_iota(jnp.int32, (OBJ, 128), 0)

    def kind(k):
        return jnp.sum(jnp.where(lane == k * OBJ, total, 0.0), axis=1, keepdims=True)

    norm_old, curvature, cross, square = kind(0), kind(1), kind(2), kind(3)
    step_len = norm_old / curvature
    norm_new = jnp.maximum(norm_old - 2.0 * step_len * cross + step_len * step_len * square, 0.0)
    ratio_new = norm_new / (norm_old + 1e-06)
    d = kept[0]
    solution_new[...] = kept[2] + step_len * d
    moved = kept[1] - step_len * image[...]
    residual_new[...] = moved
    direction_new[...] = moved + ratio_new * d


def f32(*shape):
    return jax.ShapeDtypeStruct(shape, jnp.float32)


def bf16(*shape):
    return jax.ShapeDtypeStruct(shape, jnp.bfloat16)


def exchanged(x, axis):
    return lax.all_to_all(x, axis, 0, 0)


def from_ahead(x, axis, by):
    length = lax.axis_size(axis)
    return lax.ppermute(x, axis, [(i, (i - by) % length) for i in range(length)])


def shards(points, solution, residual, direction, outscale, noise_var):
    devices = math.prod(SIZES)
    place = jnp.stack([lax.axis_index(a) for a in ("y", "core", "x", "z")]).astype(jnp.int32)
    packed, own, kept = pl.pallas_call(
        pack_kernel,
        in_specs=[VMEM] * 4 + [SMEM] * 2,
        out_specs=[VMEM] * 3,
        out_shape=[bf16(BLOCKS, PACK, WIDTH), bf16(1, PACK, WIDTH), f32(5, OBJ, WIDTH)],
    )(points, direction, residual, solution, outscale, noise_var)
    pair = jnp.concatenate([own, from_ahead(own, "core", 1)], axis=0)
    rows = [pair] + [from_ahead(pair, "y", -k) for k in (1, 2, 3)]
    cols = exchanged(packed, "z")
    cols1, cols2 = from_ahead(cols, "x", 1), from_ahead(cols, "x", 2)
    ax, dr, row_acc, col_near = pl.pallas_call(
        near_kernel,
        in_specs=[SMEM] + [VMEM] * 5,
        out_specs=[VMEM] * 4,
        out_shape=[
            bf16(DEPTH, LANES),
            bf16(16, LANES + HALF),
            f32(16, LANES),
            f32(BLOCKS, OBJ, WIDTH),
        ],
        scratch_shapes=[
            pltpu.VMEM((BLOCKS, PACK, WIDTH), jnp.bfloat16),
            pltpu.VMEM((5, WIDTH, DEPTH), jnp.bfloat16),
            pltpu.VMEM((5, 16, WIDTH), jnp.bfloat16),
            pltpu.VMEM((5, 16, WIDTH), jnp.float32),
        ]
        + stages(),
        compiler_params=params(),
        cost_estimate=pl.CostEstimate(flops=8 * 10**9, bytes_accessed=10**6, transcendentals=10**7),
    )(place, *rows, cols)
    by_rows, col1, col2 = pl.pallas_call(
        far_kernel,
        in_specs=[SMEM] + [VMEM] * 5,
        out_specs=[VMEM] * 3,
        out_shape=[f32(BLOCKS, OBJ, WIDTH)] * 3,
        scratch_shapes=[
            pltpu.VMEM((16, LANES), jnp.float32),
            pltpu.VMEM((12, WIDTH, DEPTH), jnp.bfloat16),
            pltpu.VMEM((12, 16, WIDTH), jnp.bfloat16),
            pltpu.VMEM((12, 16, WIDTH), jnp.float32),
        ]
        + stages(),
        compiler_params=params(),
        cost_estimate=pl.CostEstimate(flops=24 * 10**9, bytes_accessed=10**6, transcendentals=10**7),
    )(place, ax, dr, row_acc, cols1, cols2)
    col1, col2 = from_ahead(col1, "x", -1), from_ahead(col2, "x", -2)
    by_rows = exchanged(by_rows, GROUP)
    by_cols = pl.pallas_call(
        join_kernel,
        in_specs=[VMEM] * 3,
        out_specs=VMEM,
        out_shape=f32(BLOCKS, OBJ, WIDTH),
        compiler_params=params(4),
    )(col_near, col1, col2)
    by_cols = exchanged(by_cols, "z")
    image, sums = pl.pallas_call(
        image_kernel,
        in_specs=[VMEM] * 3,
        out_specs=[VMEM] * 2,
        out_shape=[f32(OBJ, WIDTH), f32(devices, 128)],
        compiler_params=params(4),
    )(by_rows, by_cols, kept)
    sums = exchanged(sums.reshape(devices, 1, 128), AXES).reshape(devices, 128)
    return pl.pallas_call(
        update_kernel,
        in_specs=[VMEM] * 3,
        out_specs=[VMEM] * 3,
        out_shape=[f32(OBJ, WIDTH)] * 3,
        compiler_params=params(4),
    )(sums, kept, image)


def solution(mesh):
    own = Mesh(mesh.devices.reshape(SIZES), AXES)
    split = P(None, AXES)
    return jax.shard_map(
        shards,
        mesh=own,
        in_specs=(split, split, split, split, P(), P()),
        out_specs=(split, split, split),
        check_vma=False,
    )
```

```python
import functools
import math

import jax
import jax.numpy as jnp
from jax import lax
from jax.experimental import pallas as pl
from jax.experimental.pallas import tpu as pltpu
from jax.sharding import Mesh
from jax.sharding import PartitionSpec as P

SIZES = (4, 4, 2, 8)
AXES = ("y", "x", "core", "z")
GROUP = ("y", "core")
IN, OBJ, WIDTH = 32, 4, 384
BLOCKS = 8
LANES = BLOCKS * WIDTH
HALF = LANES // 2
DEPTH = 128
PACK = 48
LOG2E = 1.0 / math.log(2.0)
SCALE = 5.0 / 9.0
VMEM = pl.BlockSpec(memory_space=pltpu.VMEM)
SMEM = pl.BlockSpec(memory_space=pltpu.SMEM)


def params(mebibytes=48):
    return pltpu.CompilerParams(vmem_limit_bytes=mebibytes * 1024 * 1024)


def parts(x, count):
    out = []
    for _ in range(count):
        out.append(x.astype(jnp.bfloat16).astype(jnp.float32))
        x = x - out[-1]
    return out


def rows_of(values, shape):
    where = lax.broadcasted_iota(jnp.int32, shape, 0)
    out = jnp.zeros(shape, jnp.float32)
    for i, value in enumerate(values):
        out = jnp.where(where == i, value, out)
    return out


def row_features(pts):
    wide = pts.astype(jnp.float32)
    own = SCALE * jnp.sum(wide * wide, axis=0, keepdims=True)
    extra = rows_of([1.0] * 3 + parts(own, 3), (16, WIDTH))
    zeros = jnp.zeros((16, WIDTH), jnp.float32)
    whole = jnp.concatenate(parts((-2.0 * SCALE) * wide, 3) + [extra, zeros], axis=0)
    return whole.astype(jnp.bfloat16)


def col_features(pts):
    wide = pts.astype(jnp.float32)
    own = SCALE * jnp.sum(wide * wide, axis=0, keepdims=True)
    extra = rows_of(parts(own, 3) + [1.0] * 3, (16, WIDTH))
    zeros = jnp.zeros((16, WIDTH), jnp.float32)
    whole = jnp.concatenate([wide, wide, wide, extra, zeros], axis=0)
    return whole.T.astype(jnp.bfloat16)


def dot(a, b, dims=((1,), (0,))):
    return lax.dot_general(a, b, (dims, ((), ())), preferred_element_type=jnp.float32)


def weights(sq):
    sq = jnp.maximum(sq, 1e-30)
    v = sq * lax.rsqrt(sq)
    w = ((sq + v) + 1.0 / 3.0) * jnp.exp2(v * (-3.0 * LOG2E))
    hi = w.astype(jnp.bfloat16)
    lo = ((w - hi.astype(jnp.float32)) * LOW).astype(FINE)
    return hi, lo


def both(a, hi, lo, dims=((1,), (0,))):
    return dot(a[0], hi, dims) + (1.0 / LOW) * dot(a[1], lo, dims)


def fine(tail):
    wide = folded(tail.astype(jnp.float32))
    high = wide.astype(FINE).astype(jnp.float32)
    zeros = jnp.zeros((16 - 2 * OBJ, wide.shape[1]), jnp.float32)
    return jnp.concatenate([high, wide - high, zeros], axis=0).astype(FINE)


TRANSPOSED = ((1,), (1,))
STRIP = 256
LOW = 2.0**14
FINE = jnp.float8_e4m3fn


def pipeline(count, spare, place_of, bt, ax, dr, dr8, dc, dc8, row_acc, col_acc, stages):
    xa, xb, ha, hb, la, lb = stages

    def distances(step, out, o):
        i, at, _ = place_of(step)
        out[:, o : o + STRIP] = dot(bt[i], ax[:, pl.ds(pl.multiple_of(at + o, 128), STRIP)])

    def by_col(step, hi, lo, o):
        _, _, at = place_of(step)
        lanes = pl.ds(pl.multiple_of(at + o, 128), STRIP)
        return both((dr[:, lanes], dr8[:, lanes]), hi[:, o : o + STRIP], lo[:, o : o + STRIP], TRANSPOSED)

    def by_row(step, hi, lo, o, first):
        i, at, _ = place_of(step)
        lanes = pl.ds(pl.multiple_of(jnp.where(first, LANES, at) + o, 128), STRIP)
        row_acc[:, lanes] += both((dc[i], dc8[i]), hi[:, o : o + STRIP], lo[:, o : o + STRIP])

    def half(step, x, x_next, hi, lo, hi_last, lo_last):
        last, following = jnp.maximum(step - 1, 0), jnp.minimum(step + 1, count - 1)
        total = None
        for o in range(0, HALF, STRIP):
            distances(following, x_next, o)
            part = by_col(last, hi_last, lo_last, o)
            total = part if total is None else total + part
            by_row(last, hi_last, lo_last, o, step == 0)
            got = weights(x[:, o : o + STRIP])
            hi[:, o : o + STRIP], lo[:, o : o + STRIP] = got
        col_acc[jnp.where(step == 0, spare, place_of(last)[0])] += total

    for o in range(0, HALF, STRIP):
        distances(0, xa, o)

    @pl.loop(0, count // 2)
    def _(pair):
        half(2 * pair, xa, xb, ha, la, hb, lb)
        half(2 * pair + 1, xb, xa, hb, lb, ha, la)

    total = None
    for o in range(0, HALF, STRIP):
        part = by_col(count - 1, hb, lb, o)
        total = part if total is None else total + part
        by_row(count - 1, hb, lb, o, False)
    col_acc[place_of(count - 1)[0]] += total


def stages():
    block = (WIDTH, HALF)
    return [pltpu.VMEM(block, jnp.float32)] * 2 + [pltpu.VMEM(block, jnp.bfloat16)] * 2 + [pltpu.VMEM(block, FINE)] * 2


def folded(x):
    return x[:OBJ] + x[OBJ : 2 * OBJ]


def pack_kernel(points, direction, residual, solution, outscale, noise, out, own, kept):
    wide = direction[...]
    high, low = parts(wide, 2)
    tail = jnp.concatenate([high, low, jnp.zeros((8, WIDTH), jnp.float32)], axis=0)
    tail = tail.astype(jnp.bfloat16)
    own[0, :IN, :] = points[...]
    own[0, IN:, :] = tail
    for i in range(BLOCKS):
        out[i, :IN, :] = points[...]
        out[i, IN:, :] = tail
    kept[0] = wide
    kept[1] = residual[...]
    kept[2] = solution[...]
    for o in range(OBJ):
        kept[3, o : o + 1, :] = jnp.full((1, WIDTH), 3.0 * outscale[o], jnp.float32)
        kept[4, o : o + 1, :] = jnp.full((1, WIDTH), noise[o], jnp.float32)


def near_kernel(place, r0, r1, r2, r3, cols, ax, dr, dr8, row_out, col_near, row_acc, rows, bt, dc, dc8, col_acc, *work):
    y, core, z = place[0], place[1], place[3]
    h = 2 * y + core
    for k, ref in enumerate((r0, r1, r2, r3)):
        rows[2 * k] = ref[0]
        rows[2 * k + 1] = ref[1]
    for i in range(BLOCKS):
        there = lax.rem(h + i, BLOCKS)
        away = lax.rem(y - there // 2 + 4, 4)
        other = jnp.where(lax.rem(there, 2) == core, 0, 1)
        block = rows[2 * away + other]
        lanes = pl.ds(i * WIDTH, WIDTH)
        ax[:, lanes] = row_features(block[:IN])
        tail = block[IN:]
        tail8 = fine(tail)
        dr[:, lanes], dr8[:, lanes] = tail, tail8
        if i < BLOCKS // 2:
            lanes = pl.ds(LANES + i * WIDTH, WIDTH)
            dr[:, lanes] = jnp.zeros_like(tail) if i == 0 else tail
            dr8[:, lanes] = jnp.zeros_like(tail8) if i == 0 else tail8
    row_acc[...] = jnp.zeros_like(row_acc)
    col_acc[...] = jnp.zeros_like(col_acc)
    for i in range(5):
        block = cols[lax.rem(z + i, BLOCKS)]
        bt[i] = col_features(block[:IN])
        dc[i], dc8[i] = block[IN:], fine(block[IN:])
    tie = jnp.where(z < BLOCKS // 2, 0, WIDTH)

    def place_of(s):
        i = jnp.where(s < 6, 1 + s // 2, jnp.where(s == 6, 4, 0))
        at = jnp.where(s < 6, lax.rem(s, 2) * HALF, jnp.where(s == 6, tie, 0))
        return i, at, jnp.where(s == 7, LANES, at)

    pipeline(8, 5, place_of, bt, ax, dr, dr8, dc, dc8, row_acc, col_acc, work)

    lanes = pl.ds(HALF, WIDTH)
    hi, lo = weights(dot(bt[0], ax[:, lanes]))
    row_acc[:, lanes] += both((dc[0], dc8[0]), hi, lo)
    row_out[...] = row_acc[:, :LANES]
    for i in range(BLOCKS):
        got = folded(col_acc[i]) if i < 5 else jnp.zeros((OBJ, WIDTH), jnp.float32)
        col_near[lax.rem(z + i, BLOCKS)] = got


def far_kernel(place, ax, dr, dr8, row_in, cols1, cols2, row_out, col1, col2, row_acc, bt, dc, dc8, col_acc, *work):
    y, core, x, z = place[0], place[1], place[2], place[3]
    h = 2 * y + core
    row_acc[:, :LANES] = row_in[...]
    col_acc[...] = jnp.zeros_like(col_acc)
    first = z + jnp.where(x < 2, 0, 1)
    for i in range(12):
        block = cols1[i] if i < BLOCKS else cols2[lax.rem(first + i, BLOCKS)]
        bt[i] = col_features(block[:IN])
        dc[i], dc8[i] = block[IN:], fine(block[IN:])

    def place_of(s):
        at = lax.rem(s, 2) * HALF
        return s // 2, at, at

    pipeline(24, 12, place_of, bt, ax, dr, dr8, dc, dc8, row_acc, col_acc, work)
    for i in range(BLOCKS):
        row_out[lax.rem(h + i, BLOCKS)] = folded(row_acc[:, pl.ds(i * WIDTH, WIDTH)])
        col1[i] = folded(col_acc[i])
        got = folded(col_acc[BLOCKS + i]) if i < 4 else jnp.zeros((OBJ, WIDTH), jnp.float32)
        col2[lax.rem(first + i, BLOCKS)] = got


def join_kernel(near, one, two, out):
    out[...] = near[...] + one[...] + two[...]


def image_kernel(by_rows, by_cols, kept, image, sums):
    total = jnp.zeros((OBJ, WIDTH), jnp.float32)
    for i in range(BLOCKS):
        total = total + by_rows[i] + by_cols[i]
    d, r = kept[0], kept[1]
    got = kept[3] * total + kept[4] * d
    image[...] = got
    products = jnp.concatenate([r * r, d * got, r * got, got * got], axis=0)
    column = jnp.sum(products, axis=1, keepdims=True)
    shape = (4 * OBJ, 128)
    diagonal = lax.broadcasted_iota(jnp.int32, shape, 0) == lax.broadcasted_iota(jnp.int32, shape, 1)
    row = jnp.sum(jnp.where(diagonal, column, 0.0), axis=0, keepdims=True)
    sums[...] = jnp.broadcast_to(row, sums.shape)


def update_kernel(sums, kept, image, solution_new, residual_new, direction_new):
    total = jnp.sum(sums[...], axis=0, keepdims=True)
    lane = lax.broadcasted_iota(jnp.int32, (OBJ, 128), 1) - lax.broadcasted_iota(jnp.int32, (OBJ, 128), 0)

    def kind(k):
        return jnp.sum(jnp.where(lane == k * OBJ, total, 0.0), axis=1, keepdims=True)

    norm_old, curvature, cross, square = kind(0), kind(1), kind(2), kind(3)
    step_len = norm_old / curvature
    norm_new = jnp.maximum(norm_old - 2.0 * step_len * cross + step_len * step_len * square, 0.0)
    ratio_new = norm_new / (norm_old + 1e-06)
    d = kept[0]
    solution_new[...] = kept[2] + step_len * d
    moved = kept[1] - step_len * image[...]
    residual_new[...] = moved
    direction_new[...] = moved + ratio_new * d


def f32(*shape):
    return jax.ShapeDtypeStruct(shape, jnp.float32)


def bf16(*shape):
    return jax.ShapeDtypeStruct(shape, jnp.bfloat16)


def exchanged(x, axis):
    return lax.all_to_all(x, axis, 0, 0)


def from_ahead(x, axis, by):
    length = lax.axis_size(axis)
    return lax.ppermute(x, axis, [(i, (i - by) % length) for i in range(length)])


def shards(points, solution, residual, direction, outscale, noise_var):
    devices = math.prod(SIZES)
    place = jnp.stack([lax.axis_index(a) for a in ("y", "core", "x", "z")]).astype(jnp.int32)
    packed, own, kept = pl.pallas_call(
        pack_kernel,
        in_specs=[VMEM] * 4 + [SMEM] * 2,
        out_specs=[VMEM] * 3,
        out_shape=[bf16(BLOCKS, PACK, WIDTH), bf16(1, PACK, WIDTH), f32(5, OBJ, WIDTH)],
    )(points, direction, residual, solution, outscale, noise_var)
    pair = jnp.concatenate([own, from_ahead(own, "core", 1)], axis=0)
    rows = [pair] + [from_ahead(pair, "y", -k) for k in (1, 2, 3)]
    cols = exchanged(packed, "z")
    cols1, cols2 = from_ahead(cols, "x", 1), from_ahead(cols, "x", 2)
    ax, dr, dr8, row_acc, col_near = pl.pallas_call(
        near_kernel,
        in_specs=[SMEM] + [VMEM] * 5,
        out_specs=[VMEM] * 5,
        out_shape=[
            bf16(DEPTH, LANES),
            bf16(16, LANES + HALF),
            jax.ShapeDtypeStruct((16, LANES + HALF), FINE),
            f32(16, LANES),
            f32(BLOCKS, OBJ, WIDTH),
        ],
        scratch_shapes=[
            pltpu.VMEM((16, LANES + HALF), jnp.float32),
            pltpu.VMEM((BLOCKS, PACK, WIDTH), jnp.bfloat16),
            pltpu.VMEM((5, WIDTH, DEPTH), jnp.bfloat16),
            pltpu.VMEM((5, 16, WIDTH), jnp.bfloat16),
            pltpu.VMEM((5, 16, WIDTH), FINE),
            pltpu.VMEM((6, 16, WIDTH), jnp.float32),
        ]
        + stages(),
        compiler_params=params(),
        cost_estimate=pl.CostEstimate(flops=8 * 10**9, bytes_accessed=10**6, transcendentals=10**7),
    )(place, *rows, cols)
    by_rows, col1, col2 = pl.pallas_call(
        far_kernel,
        in_specs=[SMEM] + [VMEM] * 6,
        out_specs=[VMEM] * 3,
        out_shape=[f32(BLOCKS, OBJ, WIDTH)] * 3,
        scratch_shapes=[
            pltpu.VMEM((16, LANES + HALF), jnp.float32),
            pltpu.VMEM((12, WIDTH, DEPTH), jnp.bfloat16),
            pltpu.VMEM((12, 16, WIDTH), jnp.bfloat16),
            pltpu.VMEM((12, 16, WIDTH), FINE),
            pltpu.VMEM((13, 16, WIDTH), jnp.float32),
        ]
        + stages(),
        compiler_params=params(),
        cost_estimate=pl.CostEstimate(flops=24 * 10**9, bytes_accessed=10**6, transcendentals=10**7),
    )(place, ax, dr, dr8, row_acc, cols1, cols2)
    col1, col2 = from_ahead(col1, "x", -1), from_ahead(col2, "x", -2)
    by_rows = exchanged(by_rows, GROUP)
    by_cols = pl.pallas_call(
        join_kernel,
        in_specs=[VMEM] * 3,
        out_specs=VMEM,
        out_shape=f32(BLOCKS, OBJ, WIDTH),
        compiler_params=params(4),
    )(col_near, col1, col2)
    by_cols = exchanged(by_cols, "z")
    image, sums = pl.pallas_call(
        image_kernel,
        in_specs=[VMEM] * 3,
        out_specs=[VMEM] * 2,
        out_shape=[f32(OBJ, WIDTH), f32(devices, 128)],
        compiler_params=params(4),
    )(by_rows, by_cols, kept)
    sums = exchanged(sums.reshape(devices, 1, 128), AXES).reshape(devices, 128)
    return pl.pallas_call(
        update_kernel,
        in_specs=[VMEM] * 3,
        out_specs=[VMEM] * 3,
        out_shape=[f32(OBJ, WIDTH)] * 3,
        compiler_params=params(4),
    )(sums, kept, image)


def solution(mesh):
    own = Mesh(mesh.devices.reshape(SIZES), AXES)
    split = P(None, AXES)
    return jax.shard_map(
        shards,
        mesh=own,
        in_specs=(split, split, split, split, P(), P()),
        out_specs=(split, split, split),
        check_vma=False,
    )
```

```python
import functools
import math

import jax
import jax.numpy as jnp
from jax import lax
from jax.experimental import pallas as pl
from jax.experimental.pallas import tpu as pltpu
from jax.sharding import Mesh
from jax.sharding import PartitionSpec as P

SIZES = (4, 4, 2, 8)
AXES = ("y", "x", "core", "z")
GROUP = ("y", "core")
IN, OBJ, WIDTH = 32, 4, 384
BLOCKS = 8
LANES = BLOCKS * WIDTH
HALF = LANES // 2
DEPTH = 128
PACK = 48
LOG2E = 1.0 / math.log(2.0)
SCALE = 5.0 / 9.0
VMEM = pl.BlockSpec(memory_space=pltpu.VMEM)
SMEM = pl.BlockSpec(memory_space=pltpu.SMEM)


def params(mebibytes=48):
    return pltpu.CompilerParams(vmem_limit_bytes=mebibytes * 1024 * 1024)


def parts(x, count):
    out = []
    for _ in range(count):
        out.append(x.astype(jnp.bfloat16).astype(jnp.float32))
        x = x - out[-1]
    return out


def rows_of(values, shape):
    where = lax.broadcasted_iota(jnp.int32, shape, 0)
    out = jnp.zeros(shape, jnp.float32)
    for i, value in enumerate(values):
        out = jnp.where(where == i, value, out)
    return out


def row_features(pts):
    wide = pts.astype(jnp.float32)
    own = SCALE * jnp.sum(wide * wide, axis=0, keepdims=True)
    extra = rows_of([1.0] * 3 + parts(own, 3), (16, WIDTH))
    zeros = jnp.zeros((16, WIDTH), jnp.float32)
    whole = jnp.concatenate(parts((-2.0 * SCALE) * wide, 3) + [extra, zeros], axis=0)
    return whole.astype(jnp.bfloat16)


def col_features(pts):
    wide = pts.astype(jnp.float32)
    own = SCALE * jnp.sum(wide * wide, axis=0, keepdims=True)
    extra = rows_of(parts(own, 3) + [1.0] * 3, (16, WIDTH))
    zeros = jnp.zeros((16, WIDTH), jnp.float32)
    whole = jnp.concatenate([wide, wide, wide, extra, zeros], axis=0)
    return whole.T.astype(jnp.bfloat16)


def dot(a, b, dims=((1,), (0,))):
    return lax.dot_general(a, b, (dims, ((), ())), preferred_element_type=jnp.float32)


def weights(sq):
    sq = jnp.maximum(sq, 1e-30)
    v = sq * lax.rsqrt(sq)
    w = ((sq + v) + 1.0 / 3.0) * jnp.exp2(v * (-3.0 * LOG2E))
    hi = w.astype(jnp.bfloat16)
    lo = ((w - hi.astype(jnp.float32)) * LOW).astype(FINE)
    return hi, lo


def both(a, hi, lo, dims=((1,), (0,))):
    return dot(a[0], hi, dims)[: 2 * OBJ], dot(a[1], lo, dims)[: 2 * OBJ]


def joined(high, low):
    return high + (1.0 / LOW) * low


def fine(tail):
    wide = folded(tail.astype(jnp.float32))
    high = wide.astype(FINE).astype(jnp.float32)
    zeros = jnp.zeros((16 - 2 * OBJ, wide.shape[1]), jnp.float32)
    return jnp.concatenate([high, wide - high, zeros], axis=0).astype(FINE)


TRANSPOSED = ((1,), (1,))
STRIP = 256
LOW = 2.0**14
FINE = jnp.float8_e4m3fn


def pipeline(count, spare, place_of, bt, ax, dr, dr8, dc, dc8, row_acc, col_acc, stages):
    xa, xb, ha, hb, la, lb = stages

    def distances(step, out, o):
        i, at, _ = place_of(step)
        out[:, o : o + STRIP] = dot(bt[i], ax[:, pl.ds(pl.multiple_of(at + o, 128), STRIP)])

    def by_col(step, hi, lo, o):
        _, _, at = place_of(step)
        lanes = pl.ds(pl.multiple_of(at + o, 128), STRIP)
        return both((dr[:, lanes], dr8[:, lanes]), hi[:, o : o + STRIP], lo[:, o : o + STRIP], TRANSPOSED)

    def by_row(step, hi, lo, o, first):
        i, at, _ = place_of(step)
        lanes = pl.ds(pl.multiple_of(jnp.where(first, LANES, at) + o, 128), STRIP)
        row_acc[:, lanes] += joined(*both((dc[i], dc8[i]), hi[:, o : o + STRIP], lo[:, o : o + STRIP]))

    def half(step, x, x_next, hi, lo, hi_last, lo_last):
        last, following = jnp.maximum(step - 1, 0), jnp.minimum(step + 1, count - 1)
        total = None
        for o in range(0, HALF, STRIP):
            distances(following, x_next, o)
            part = by_col(last, hi_last, lo_last, o)
            total = part if total is None else (total[0] + part[0], total[1] + part[1])
            by_row(last, hi_last, lo_last, o, step == 0)
            got = weights(x[:, o : o + STRIP])
            hi[:, o : o + STRIP], lo[:, o : o + STRIP] = got
        col_acc[jnp.where(step == 0, spare, place_of(last)[0])] += joined(*total)

    for o in range(0, HALF, STRIP):
        distances(0, xa, o)

    @pl.loop(0, count // 2)
    def _(pair):
        half(2 * pair, xa, xb, ha, la, hb, lb)
        half(2 * pair + 1, xb, xa, hb, lb, ha, la)

    total = None
    for o in range(0, HALF, STRIP):
        part = by_col(count - 1, hb, lb, o)
        total = part if total is None else (total[0] + part[0], total[1] + part[1])
        by_row(count - 1, hb, lb, o, False)
    col_acc[place_of(count - 1)[0]] += joined(*total)


def stages():
    block = (WIDTH, HALF)
    return [pltpu.VMEM(block, jnp.float32)] * 2 + [pltpu.VMEM(block, jnp.bfloat16)] * 2 + [pltpu.VMEM(block, FINE)] * 2


def folded(x):
    return x[:OBJ] + x[OBJ : 2 * OBJ]


def pack_kernel(points, direction, residual, solution, outscale, noise, out, own, kept):
    wide = direction[...]
    high, low = parts(wide, 2)
    tail = jnp.concatenate([high, low, jnp.zeros((8, WIDTH), jnp.float32)], axis=0)
    tail = tail.astype(jnp.bfloat16)
    own[0, :IN, :] = points[...]
    own[0, IN:, :] = tail
    for i in range(BLOCKS):
        out[i, :IN, :] = points[...]
        out[i, IN:, :] = tail
    kept[0] = wide
    kept[1] = residual[...]
    kept[2] = solution[...]
    for o in range(OBJ):
        kept[3, o : o + 1, :] = jnp.full((1, WIDTH), 3.0 * outscale[o], jnp.float32)
        kept[4, o : o + 1, :] = jnp.full((1, WIDTH), noise[o], jnp.float32)


def near_kernel(place, r0, r1, r2, r3, cols, ax, dr, dr8, row_out, col_near, row_acc, rows, bt, dc, dc8, col_acc, *work):
    y, core, z = place[0], place[1], place[3]
    h = 2 * y + core
    for k, ref in enumerate((r0, r1, r2, r3)):
        rows[2 * k] = ref[0]
        rows[2 * k + 1] = ref[1]
    for i in range(BLOCKS):
        there = lax.rem(h + i, BLOCKS)
        away = lax.rem(y - there // 2 + 4, 4)
        other = jnp.where(lax.rem(there, 2) == core, 0, 1)
        block = rows[2 * away + other]
        lanes = pl.ds(i * WIDTH, WIDTH)
        ax[:, lanes] = row_features(block[:IN])
        tail = block[IN:]
        tail8 = fine(tail)
        dr[:, lanes], dr8[:, lanes] = tail, tail8
        if i < BLOCKS // 2:
            lanes = pl.ds(LANES + i * WIDTH, WIDTH)
            dr[:, lanes] = jnp.zeros_like(tail) if i == 0 else tail
            dr8[:, lanes] = jnp.zeros_like(tail8) if i == 0 else tail8
    row_acc[...] = jnp.zeros_like(row_acc)
    col_acc[...] = jnp.zeros_like(col_acc)
    for i in range(5):
        block = cols[lax.rem(z + i, BLOCKS)]
        bt[i] = col_features(block[:IN])
        dc[i], dc8[i] = block[IN:], fine(block[IN:])
    tie = jnp.where(z < BLOCKS // 2, 0, WIDTH)

    def place_of(s):
        i = jnp.where(s < 6, 1 + s // 2, jnp.where(s == 6, 4, 0))
        at = jnp.where(s < 6, lax.rem(s, 2) * HALF, jnp.where(s == 6, tie, 0))
        return i, at, jnp.where(s == 7, LANES, at)

    pipeline(8, 5, place_of, bt, ax, dr, dr8, dc, dc8, row_acc, col_acc, work)

    lanes = pl.ds(HALF, WIDTH)
    hi, lo = weights(dot(bt[0], ax[:, lanes]))
    row_acc[:, lanes] += joined(*both((dc[0], dc8[0]), hi, lo))
    row_out[...] = row_acc[:, :LANES]
    for i in range(BLOCKS):
        got = folded(col_acc[i]) if i < 5 else jnp.zeros((OBJ, WIDTH), jnp.float32)
        col_near[lax.rem(z + i, BLOCKS)] = got


def far_kernel(place, ax, dr, dr8, row_in, cols1, cols2, row_out, col1, col2, row_acc, bt, dc, dc8, col_acc, *work):
    y, core, x, z = place[0], place[1], place[2], place[3]
    h = 2 * y + core
    row_acc[:, :LANES] = row_in[...]
    col_acc[...] = jnp.zeros_like(col_acc)
    first = z + jnp.where(x < 2, 0, 1)
    for i in range(12):
        block = cols1[i] if i < BLOCKS else cols2[lax.rem(first + i, BLOCKS)]
        bt[i] = col_features(block[:IN])
        dc[i], dc8[i] = block[IN:], fine(block[IN:])

    def place_of(s):
        at = lax.rem(s, 2) * HALF
        return s // 2, at, at

    pipeline(24, 12, place_of, bt, ax, dr, dr8, dc, dc8, row_acc, col_acc, work)
    for i in range(BLOCKS):
        row_out[lax.rem(h + i, BLOCKS)] = folded(row_acc[:, pl.ds(i * WIDTH, WIDTH)])
        col1[i] = folded(col_acc[i])
        got = folded(col_acc[BLOCKS + i]) if i < 4 else jnp.zeros((OBJ, WIDTH), jnp.float32)
        col2[lax.rem(first + i, BLOCKS)] = got


def join_kernel(near, one, two, out):
    out[...] = near[...] + one[...] + two[...]


def image_kernel(by_rows, by_cols, kept, image, sums):
    total = jnp.zeros((OBJ, WIDTH), jnp.float32)
    for i in range(BLOCKS):
        total = total + by_rows[i] + by_cols[i]
    d, r = kept[0], kept[1]
    got = kept[3] * total + kept[4] * d
    image[...] = got
    products = jnp.concatenate([r * r, d * got, r * got, got * got], axis=0)
    column = jnp.sum(products, axis=1, keepdims=True)
    shape = (4 * OBJ, 128)
    diagonal = lax.broadcasted_iota(jnp.int32, shape, 0) == lax.broadcasted_iota(jnp.int32, shape, 1)
    row = jnp.sum(jnp.where(diagonal, column, 0.0), axis=0, keepdims=True)
    sums[...] = jnp.broadcast_to(row, sums.shape)


def update_kernel(sums, kept, image, solution_new, residual_new, direction_new):
    total = jnp.sum(sums[...], axis=0, keepdims=True)
    lane = lax.broadcasted_iota(jnp.int32, (OBJ, 128), 1) - lax.broadcasted_iota(jnp.int32, (OBJ, 128), 0)

    def kind(k):
        return jnp.sum(jnp.where(lane == k * OBJ, total, 0.0), axis=1, keepdims=True)

    norm_old, curvature, cross, square = kind(0), kind(1), kind(2), kind(3)
    step_len = norm_old / curvature
    norm_new = jnp.maximum(norm_old - 2.0 * step_len * cross + step_len * step_len * square, 0.0)
    ratio_new = norm_new / (norm_old + 1e-06)
    d = kept[0]
    solution_new[...] = kept[2] + step_len * d
    moved = kept[1] - step_len * image[...]
    residual_new[...] = moved
    direction_new[...] = moved + ratio_new * d


def f32(*shape):
    return jax.ShapeDtypeStruct(shape, jnp.float32)


def bf16(*shape):
    return jax.ShapeDtypeStruct(shape, jnp.bfloat16)


def exchanged(x, axis):
    return lax.all_to_all(x, axis, 0, 0)


def from_ahead(x, axis, by):
    length = lax.axis_size(axis)
    return lax.ppermute(x, axis, [(i, (i - by) % length) for i in range(length)])


def shards(points, solution, residual, direction, outscale, noise_var):
    devices = math.prod(SIZES)
    place = jnp.stack([lax.axis_index(a) for a in ("y", "core", "x", "z")]).astype(jnp.int32)
    packed, own, kept = pl.pallas_call(
        pack_kernel,
        in_specs=[VMEM] * 4 + [SMEM] * 2,
        out_specs=[VMEM] * 3,
        out_shape=[bf16(BLOCKS, PACK, WIDTH), bf16(1, PACK, WIDTH), f32(5, OBJ, WIDTH)],
    )(points, direction, residual, solution, outscale, noise_var)
    pair = jnp.concatenate([own, from_ahead(own, "core", 1)], axis=0)
    rows = [pair] + [from_ahead(pair, "y", -k) for k in (1, 2, 3)]
    cols = exchanged(packed, "z")
    cols1, cols2 = from_ahead(cols, "x", 1), from_ahead(cols, "x", 2)
    ax, dr, dr8, row_acc, col_near = pl.pallas_call(
        near_kernel,
        in_specs=[SMEM] + [VMEM] * 5,
        out_specs=[VMEM] * 5,
        out_shape=[
            bf16(DEPTH, LANES),
            bf16(16, LANES + HALF),
            jax.ShapeDtypeStruct((16, LANES + HALF), FINE),
            f32(2 * OBJ, LANES),
            f32(BLOCKS, OBJ, WIDTH),
        ],
        scratch_shapes=[
            pltpu.VMEM((2 * OBJ, LANES + HALF), jnp.float32),
            pltpu.VMEM((BLOCKS, PACK, WIDTH), jnp.bfloat16),
            pltpu.VMEM((5, WIDTH, DEPTH), jnp.bfloat16),
            pltpu.VMEM((5, 16, WIDTH), jnp.bfloat16),
            pltpu.VMEM((5, 16, WIDTH), FINE),
            pltpu.VMEM((6, 2 * OBJ, WIDTH), jnp.float32),
        ]
        + stages(),
        compiler_params=params(),
        cost_estimate=pl.CostEstimate(flops=8 * 10**9, bytes_accessed=10**6, transcendentals=10**7),
    )(place, *rows, cols)
    by_rows, col1, col2 = pl.pallas_call(
        far_kernel,
        in_specs=[SMEM] + [VMEM] * 6,
        out_specs=[VMEM] * 3,
        out_shape=[f32(BLOCKS, OBJ, WIDTH)] * 3,
        scratch_shapes=[
            pltpu.VMEM((2 * OBJ, LANES + HALF), jnp.float32),
            pltpu.VMEM((12, WIDTH, DEPTH), jnp.bfloat16),
            pltpu.VMEM((12, 16, WIDTH), jnp.bfloat16),
            pltpu.VMEM((12, 16, WIDTH), FINE),
            pltpu.VMEM((13, 2 * OBJ, WIDTH), jnp.float32),
        ]
        + stages(),
        compiler_params=params(),
        cost_estimate=pl.CostEstimate(flops=24 * 10**9, bytes_accessed=10**6, transcendentals=10**7),
    )(place, ax, dr, dr8, row_acc, cols1, cols2)
    col1, col2 = from_ahead(col1, "x", -1), from_ahead(col2, "x", -2)
    by_rows = exchanged(by_rows, GROUP)
    by_cols = pl.pallas_call(
        join_kernel,
        in_specs=[VMEM] * 3,
        out_specs=VMEM,
        out_shape=f32(BLOCKS, OBJ, WIDTH),
        compiler_params=params(4),
    )(col_near, col1, col2)
    by_cols = exchanged(by_cols, "z")
    image, sums = pl.pallas_call(
        image_kernel,
        in_specs=[VMEM] * 3,
        out_specs=[VMEM] * 2,
        out_shape=[f32(OBJ, WIDTH), f32(devices, 128)],
        compiler_params=params(4),
    )(by_rows, by_cols, kept)
    sums = exchanged(sums.reshape(devices, 1, 128), AXES).reshape(devices, 128)
    return pl.pallas_call(
        update_kernel,
        in_specs=[VMEM] * 3,
        out_specs=[VMEM] * 3,
        out_shape=[f32(OBJ, WIDTH)] * 3,
        compiler_params=params(4),
    )(sums, kept, image)


def solution(mesh):
    own = Mesh(mesh.devices.reshape(SIZES), AXES)
    split = P(None, AXES)
    return jax.shard_map(
        shards,
        mesh=own,
        in_specs=(split, split, split, split, P(), P()),
        out_specs=(split, split, split),
        check_vma=False,
    )
```

```python
import functools
import math

import jax
import jax.numpy as jnp
from jax import lax
from jax.experimental import pallas as pl
from jax.experimental.pallas import tpu as pltpu
from jax.sharding import Mesh
from jax.sharding import PartitionSpec as P

SIZES = (4, 4, 2, 8)
AXES = ("y", "x", "core", "z")
GROUP = ("y", "core")
IN, OBJ, WIDTH = 32, 4, 384
BLOCKS = 8
LANES = BLOCKS * WIDTH
HALF = LANES // 2
DEPTH = 128
PACK = 48
LOG2E = 1.0 / math.log(2.0)
SCALE = 5.0 / 9.0
VMEM = pl.BlockSpec(memory_space=pltpu.VMEM)
SMEM = pl.BlockSpec(memory_space=pltpu.SMEM)


def params(mebibytes=48):
    return pltpu.CompilerParams(vmem_limit_bytes=mebibytes * 1024 * 1024)


def parts(x, count):
    out = []
    for _ in range(count):
        out.append(x.astype(jnp.bfloat16).astype(jnp.float32))
        x = x - out[-1]
    return out


def rows_of(values, shape):
    where = lax.broadcasted_iota(jnp.int32, shape, 0)
    out = jnp.zeros(shape, jnp.float32)
    for i, value in enumerate(values):
        out = jnp.where(where == i, value, out)
    return out


def row_features(pts):
    wide = pts.astype(jnp.float32)
    own = SCALE * jnp.sum(wide * wide, axis=0, keepdims=True)
    extra = rows_of([1.0] * 3 + parts(own, 3), (16, WIDTH))
    zeros = jnp.zeros((16, WIDTH), jnp.float32)
    whole = jnp.concatenate(parts((-2.0 * SCALE) * wide, 3) + [extra, zeros], axis=0)
    return whole.astype(jnp.bfloat16)


def col_features(pts):
    wide = pts.astype(jnp.float32)
    own = SCALE * jnp.sum(wide * wide, axis=0, keepdims=True)
    extra = rows_of(parts(own, 3) + [1.0] * 3, (16, WIDTH))
    zeros = jnp.zeros((16, WIDTH), jnp.float32)
    whole = jnp.concatenate([wide, wide, wide, extra, zeros], axis=0)
    return whole.T.astype(jnp.bfloat16)


def dot(a, b, dims=((1,), (0,))):
    return lax.dot_general(a, b, (dims, ((), ())), preferred_element_type=jnp.float32)


def weights(sq):
    sq = jnp.maximum(sq, 1e-30)
    v = sq * lax.rsqrt(sq)
    w = ((sq + v) + 1.0 / 3.0) * jnp.exp2(v * (-3.0 * LOG2E))
    hi = w.astype(jnp.bfloat16)
    lo = ((w - hi.astype(jnp.float32)) * LOW).astype(FINE)
    return hi, lo


def both(a, hi, lo, dims=((1,), (0,))):
    return dot(a[0], hi, dims)[: 2 * OBJ], dot(a[1], lo, dims)[: 2 * OBJ]


def joined(high, low):
    return high + (1.0 / LOW) * low


def fine(tail):
    wide = folded(tail.astype(jnp.float32))
    high = wide.astype(FINE).astype(jnp.float32)
    zeros = jnp.zeros((16 - 2 * OBJ, wide.shape[1]), jnp.float32)
    return jnp.concatenate([high, wide - high, zeros], axis=0).astype(FINE)


TRANSPOSED = ((1,), (1,))
STRIP = 256
LOW = 2.0**14
FINE = jnp.float8_e4m3fn


def pipeline(count, spare, place_of, bt, ax, dr, dr8, dc, dc8, row_acc, col_acc, stages, early=lambda: None, late=lambda: None):
    xa, xb, ha, hb, la, lb = stages

    def distances(step, out, o):
        i, at, _ = place_of(step)
        out[:, o : o + STRIP] = dot(bt[i], ax[:, pl.ds(pl.multiple_of(at + o, 128), STRIP)])

    def by_col(step, hi, lo, o):
        _, _, at = place_of(step)
        lanes = pl.ds(pl.multiple_of(at + o, 128), STRIP)
        return both((dr[:, lanes], dr8[:, lanes]), hi[:, o : o + STRIP], lo[:, o : o + STRIP], TRANSPOSED)

    def by_row(step, hi, lo, o, first):
        i, at, _ = place_of(step)
        lanes = pl.ds(pl.multiple_of(jnp.where(first, LANES, at) + o, 128), STRIP)
        row_acc[:, lanes] += joined(*both((dc[i], dc8[i]), hi[:, o : o + STRIP], lo[:, o : o + STRIP]))

    def half(step, x, x_next, hi, lo, hi_last, lo_last):
        last, following = jnp.maximum(step - 1, 0), jnp.minimum(step + 1, count - 1)
        total = None
        for o in range(0, HALF, STRIP):
            distances(following, x_next, o)
            part = by_col(last, hi_last, lo_last, o)
            total = part if total is None else (total[0] + part[0], total[1] + part[1])
            by_row(last, hi_last, lo_last, o, step == 0)
            got = weights(x[:, o : o + STRIP])
            hi[:, o : o + STRIP], lo[:, o : o + STRIP] = got
        col_acc[jnp.where(step == 0, spare, place_of(last)[0])] += joined(*total)

    for o in range(0, HALF, STRIP):
        distances(0, xa, o)
    early()

    @pl.loop(0, count // 2)
    def _(pair):
        half(2 * pair, xa, xb, ha, la, hb, lb)
        half(2 * pair + 1, xb, xa, hb, lb, ha, la)

    late()
    total = None
    for o in range(0, HALF, STRIP):
        part = by_col(count - 1, hb, lb, o)
        total = part if total is None else (total[0] + part[0], total[1] + part[1])
        by_row(count - 1, hb, lb, o, False)
    col_acc[place_of(count - 1)[0]] += joined(*total)


def stages():
    block = (WIDTH, HALF)
    return [pltpu.VMEM(block, jnp.float32)] * 2 + [pltpu.VMEM(block, jnp.bfloat16)] * 2 + [pltpu.VMEM(block, FINE)] * 2


def folded(x):
    return x[:OBJ] + x[OBJ : 2 * OBJ]


def pack_kernel(points, direction, residual, solution, outscale, noise, out, own, kept):
    wide = direction[...]
    high, low = parts(wide, 2)
    tail = jnp.concatenate([high, low, jnp.zeros((8, WIDTH), jnp.float32)], axis=0)
    tail = tail.astype(jnp.bfloat16)
    own[0, :IN, :] = points[...]
    own[0, IN:, :] = tail
    for i in range(BLOCKS):
        out[i, :IN, :] = points[...]
        out[i, IN:, :] = tail
    kept[0] = wide
    kept[1] = residual[...]
    kept[2] = solution[...]
    for o in range(OBJ):
        kept[3, o : o + 1, :] = jnp.full((1, WIDTH), 3.0 * outscale[o], jnp.float32)
        kept[4, o : o + 1, :] = jnp.full((1, WIDTH), noise[o], jnp.float32)


def near_kernel(place, r0, r1, r2, r3, cols, ax, dr, dr8, row_out, col_near, row_acc, rows, bt, dc, dc8, col_acc, *work):
    y, core, z = place[0], place[1], place[3]
    h = 2 * y + core
    for k, ref in enumerate((r0, r1, r2, r3)):
        rows[2 * k] = ref[0]
        rows[2 * k + 1] = ref[1]
    for i in range(BLOCKS):
        there = lax.rem(h + i, BLOCKS)
        away = lax.rem(y - there // 2 + 4, 4)
        other = jnp.where(lax.rem(there, 2) == core, 0, 1)
        block = rows[2 * away + other]
        lanes = pl.ds(i * WIDTH, WIDTH)
        ax[:, lanes] = row_features(block[:IN])
        tail = block[IN:]
        tail8 = fine(tail)
        dr[:, lanes], dr8[:, lanes] = tail, tail8
        if i < BLOCKS // 2:
            lanes = pl.ds(LANES + i * WIDTH, WIDTH)
            dr[:, lanes] = jnp.zeros_like(tail) if i == 0 else tail
            dr8[:, lanes] = jnp.zeros_like(tail8) if i == 0 else tail8
    row_acc[...] = jnp.zeros_like(row_acc)
    col_acc[...] = jnp.zeros_like(col_acc)

    def features(i):
        block = cols[lax.rem(z + i, BLOCKS)]
        bt[i] = col_features(block[:IN])
        dc[i], dc8[i] = block[IN:], fine(block[IN:])

    features(1)
    tie = jnp.where(z < BLOCKS // 2, 0, WIDTH)

    def place_of(s):
        i = jnp.where(s < 6, 1 + s // 2, jnp.where(s == 6, 4, 0))
        at = jnp.where(s < 6, lax.rem(s, 2) * HALF, jnp.where(s == 6, tie, 0))
        return i, at, jnp.where(s == 7, LANES, at)

    def others():
        for i in (0, 2, 3, 4):
            features(i)

    lanes, found = pl.ds(HALF, WIDTH), []

    def fourth():
        found.extend(weights(dot(bt[0], ax[:, lanes])))

    pipeline(8, 5, place_of, bt, ax, dr, dr8, dc, dc8, row_acc, col_acc, work, others, fourth)
    hi, lo = found
    row_acc[:, lanes] += joined(*both((dc[0], dc8[0]), hi, lo))
    row_out[...] = row_acc[:, :LANES]
    for i in range(BLOCKS):
        got = folded(col_acc[i]) if i < 5 else jnp.zeros((OBJ, WIDTH), jnp.float32)
        col_near[lax.rem(z + i, BLOCKS)] = got


def far_kernel(place, ax, dr, dr8, row_in, cols1, cols2, row_out, col1, col2, row_acc, bt, dc, dc8, col_acc, *work):
    y, core, x, z = place[0], place[1], place[2], place[3]
    h = 2 * y + core
    row_acc[:, :LANES] = row_in[...]
    col_acc[...] = jnp.zeros_like(col_acc)
    first = z + jnp.where(x < 2, 0, 1)

    def features(i):
        block = cols1[i] if i < BLOCKS else cols2[lax.rem(first + i, BLOCKS)]
        bt[i] = col_features(block[:IN])
        dc[i], dc8[i] = block[IN:], fine(block[IN:])

    def others():
        for i in range(1, 12):
            features(i)

    features(0)

    def place_of(s):
        at = lax.rem(s, 2) * HALF
        return s // 2, at, at

    pipeline(24, 12, place_of, bt, ax, dr, dr8, dc, dc8, row_acc, col_acc, work, others)
    for i in range(BLOCKS):
        row_out[lax.rem(h + i, BLOCKS)] = folded(row_acc[:, pl.ds(i * WIDTH, WIDTH)])
        col1[i] = folded(col_acc[i])
        got = folded(col_acc[BLOCKS + i]) if i < 4 else jnp.zeros((OBJ, WIDTH), jnp.float32)
        col2[lax.rem(first + i, BLOCKS)] = got


def join_kernel(near, one, two, out):
    out[...] = near[...] + one[...] + two[...]


def image_kernel(by_rows, by_cols, kept, image, sums):
    total = jnp.zeros((OBJ, WIDTH), jnp.float32)
    for i in range(BLOCKS):
        total = total + by_rows[i] + by_cols[i]
    d, r = kept[0], kept[1]
    got = kept[3] * total + kept[4] * d
    image[...] = got
    products = jnp.concatenate([r * r, d * got, r * got, got * got], axis=0)
    column = jnp.sum(products, axis=1, keepdims=True)
    shape = (4 * OBJ, 128)
    diagonal = lax.broadcasted_iota(jnp.int32, shape, 0) == lax.broadcasted_iota(jnp.int32, shape, 1)
    row = jnp.sum(jnp.where(diagonal, column, 0.0), axis=0, keepdims=True)
    sums[...] = jnp.broadcast_to(row, sums.shape)


def update_kernel(sums, kept, image, solution_new, residual_new, direction_new):
    total = jnp.sum(sums[...], axis=0, keepdims=True)
    lane = lax.broadcasted_iota(jnp.int32, (OBJ, 128), 1) - lax.broadcasted_iota(jnp.int32, (OBJ, 128), 0)

    def kind(k):
        return jnp.sum(jnp.where(lane == k * OBJ, total, 0.0), axis=1, keepdims=True)

    norm_old, curvature, cross, square = kind(0), kind(1), kind(2), kind(3)
    step_len = norm_old / curvature
    norm_new = jnp.maximum(norm_old - 2.0 * step_len * cross + step_len * step_len * square, 0.0)
    ratio_new = norm_new / (norm_old + 1e-06)
    d = kept[0]
    solution_new[...] = kept[2] + step_len * d
    moved = kept[1] - step_len * image[...]
    residual_new[...] = moved
    direction_new[...] = moved + ratio_new * d


def f32(*shape):
    return jax.ShapeDtypeStruct(shape, jnp.float32)


def bf16(*shape):
    return jax.ShapeDtypeStruct(shape, jnp.bfloat16)


def exchanged(x, axis):
    return lax.all_to_all(x, axis, 0, 0)


def from_ahead(x, axis, by):
    length = lax.axis_size(axis)
    return lax.ppermute(x, axis, [(i, (i - by) % length) for i in range(length)])


def shards(points, solution, residual, direction, outscale, noise_var):
    devices = math.prod(SIZES)
    place = jnp.stack([lax.axis_index(a) for a in ("y", "core", "x", "z")]).astype(jnp.int32)
    packed, own, kept = pl.pallas_call(
        pack_kernel,
        in_specs=[VMEM] * 4 + [SMEM] * 2,
        out_specs=[VMEM] * 3,
        out_shape=[bf16(BLOCKS, PACK, WIDTH), bf16(1, PACK, WIDTH), f32(5, OBJ, WIDTH)],
    )(points, direction, residual, solution, outscale, noise_var)
    pair = jnp.concatenate([own, from_ahead(own, "core", 1)], axis=0)
    rows = [pair] + [from_ahead(pair, "y", -k) for k in (1, 2, 3)]
    cols = exchanged(packed, "z")
    cols1, cols2 = from_ahead(cols, "x", 1), from_ahead(cols, "x", 2)
    ax, dr, dr8, row_acc, col_near = pl.pallas_call(
        near_kernel,
        in_specs=[SMEM] + [VMEM] * 5,
        out_specs=[VMEM] * 5,
        out_shape=[
            bf16(DEPTH, LANES),
            bf16(16, LANES + HALF),
            jax.ShapeDtypeStruct((16, LANES + HALF), FINE),
            f32(2 * OBJ, LANES),
            f32(BLOCKS, OBJ, WIDTH),
        ],
        scratch_shapes=[
            pltpu.VMEM((2 * OBJ, LANES + HALF), jnp.float32),
            pltpu.VMEM((BLOCKS, PACK, WIDTH), jnp.bfloat16),
            pltpu.VMEM((5, WIDTH, DEPTH), jnp.bfloat16),
            pltpu.VMEM((5, 16, WIDTH), jnp.bfloat16),
            pltpu.VMEM((5, 16, WIDTH), FINE),
            pltpu.VMEM((6, 2 * OBJ, WIDTH), jnp.float32),
        ]
        + stages(),
        compiler_params=params(),
        cost_estimate=pl.CostEstimate(flops=8 * 10**9, bytes_accessed=10**6, transcendentals=10**7),
    )(place, *rows, cols)
    by_rows, col1, col2 = pl.pallas_call(
        far_kernel,
        in_specs=[SMEM] + [VMEM] * 6,
        out_specs=[VMEM] * 3,
        out_shape=[f32(BLOCKS, OBJ, WIDTH)] * 3,
        scratch_shapes=[
            pltpu.VMEM((2 * OBJ, LANES + HALF), jnp.float32),
            pltpu.VMEM((12, WIDTH, DEPTH), jnp.bfloat16),
            pltpu.VMEM((12, 16, WIDTH), jnp.bfloat16),
            pltpu.VMEM((12, 16, WIDTH), FINE),
            pltpu.VMEM((13, 2 * OBJ, WIDTH), jnp.float32),
        ]
        + stages(),
        compiler_params=params(),
        cost_estimate=pl.CostEstimate(flops=24 * 10**9, bytes_accessed=10**6, transcendentals=10**7),
    )(place, ax, dr, dr8, row_acc, cols1, cols2)
    col1, col2 = from_ahead(col1, "x", -1), from_ahead(col2, "x", -2)
    by_rows = exchanged(by_rows, GROUP)
    by_cols = pl.pallas_call(
        join_kernel,
        in_specs=[VMEM] * 3,
        out_specs=VMEM,
        out_shape=f32(BLOCKS, OBJ, WIDTH),
        compiler_params=params(4),
    )(col_near, col1, col2)
    by_cols = exchanged(by_cols, "z")
    image, sums = pl.pallas_call(
        image_kernel,
        in_specs=[VMEM] * 3,
        out_specs=[VMEM] * 2,
        out_shape=[f32(OBJ, WIDTH), f32(devices, 128)],
        compiler_params=params(4),
    )(by_rows, by_cols, kept)
    sums = exchanged(sums.reshape(devices, 1, 128), AXES).reshape(devices, 128)
    return pl.pallas_call(
        update_kernel,
        in_specs=[VMEM] * 3,
        out_specs=[VMEM] * 3,
        out_shape=[f32(OBJ, WIDTH)] * 3,
        compiler_params=params(4),
    )(sums, kept, image)


def solution(mesh):
    own = Mesh(mesh.devices.reshape(SIZES), AXES)
    split = P(None, AXES)
    return jax.shard_map(
        shards,
        mesh=own,
        in_specs=(split, split, split, split, P(), P()),
        out_specs=(split, split, split),
        check_vma=False,
    )
```

```python
import functools
import math

import jax
import jax.numpy as jnp
from jax import lax
from jax.experimental import pallas as pl
from jax.experimental.pallas import tpu as pltpu
from jax.sharding import Mesh
from jax.sharding import PartitionSpec as P

SIZES = (4, 4, 2, 8)
AXES = ("y", "x", "core", "z")
GROUP = ("y", "core")
IN, OBJ, WIDTH = 32, 4, 384
BLOCKS = 8
LANES = BLOCKS * WIDTH
HALF = LANES // 2
DEPTH = 128
PACK = 48
LOG2E = 1.0 / math.log(2.0)
SCALE = 5.0 / 9.0
VMEM = pl.BlockSpec(memory_space=pltpu.VMEM)
SMEM = pl.BlockSpec(memory_space=pltpu.SMEM)


def params(mebibytes=48):
    return pltpu.CompilerParams(vmem_limit_bytes=mebibytes * 1024 * 1024)


def parts(x, count):
    out = []
    for _ in range(count):
        out.append(x.astype(jnp.bfloat16).astype(jnp.float32))
        x = x - out[-1]
    return out


def rows_of(values, shape):
    where = lax.broadcasted_iota(jnp.int32, shape, 0)
    out = jnp.zeros(shape, jnp.float32)
    for i, value in enumerate(values):
        out = jnp.where(where == i, value, out)
    return out


def row_features(pts):
    wide = pts.astype(jnp.float32)
    own = SCALE * jnp.sum(wide * wide, axis=0, keepdims=True)
    extra = rows_of([1.0] * 3 + parts(own, 3), (16, WIDTH))
    zeros = jnp.zeros((16, WIDTH), jnp.float32)
    whole = jnp.concatenate(parts((-2.0 * SCALE) * wide, 3) + [extra, zeros], axis=0)
    return whole.astype(jnp.bfloat16)


def col_features(pts):
    wide = pts.astype(jnp.float32)
    own = SCALE * jnp.sum(wide * wide, axis=0, keepdims=True)
    extra = rows_of(parts(own, 3) + [1.0] * 3, (16, WIDTH))
    zeros = jnp.zeros((16, WIDTH), jnp.float32)
    whole = jnp.concatenate([wide, wide, wide, extra, zeros], axis=0)
    return whole.T.astype(jnp.bfloat16)


def dot(a, b, dims=((1,), (0,))):
    return lax.dot_general(a, b, (dims, ((), ())), preferred_element_type=jnp.float32)


def weights(sq):
    sq = jnp.maximum(sq, 1e-30)
    v = sq * lax.rsqrt(sq)
    w = ((sq + v) + 1.0 / 3.0) * jnp.exp2(v * (-3.0 * LOG2E))
    hi = w.astype(jnp.bfloat16)
    lo = ((w - hi.astype(jnp.float32)) * LOW).astype(FINE)
    return hi, lo


def both(a, hi, lo, dims=((1,), (0,))):
    return dot(a[0], hi, dims)[: 2 * OBJ], dot(a[1], lo, dims)[: 2 * OBJ]


def joined(high, low):
    return high + (1.0 / LOW) * low


def fine(tail):
    wide = folded(tail.astype(jnp.float32))
    high = wide.astype(FINE).astype(jnp.float32)
    zeros = jnp.zeros((16 - 2 * OBJ, wide.shape[1]), jnp.float32)
    return jnp.concatenate([high, wide - high, zeros], axis=0).astype(FINE)


TRANSPOSED = ((1,), (1,))
STRIP = 256
LOW = 2.0**14
FINE = jnp.float8_e4m3fn


def pipeline(count, spare, place_of, bt, ax, dr, dr8, dc, dc8, row_acc, col_acc, stages, early=lambda: None, late=lambda: None):
    xa, xb, ha, hb, la, lb = stages

    def distances(step, out, o):
        i, at, _ = place_of(step)
        out[:, o : o + STRIP] = dot(bt[i], ax[:, pl.ds(pl.multiple_of(at + o, 128), STRIP)])

    def by_col(step, hi, lo, o):
        _, _, at = place_of(step)
        lanes = pl.ds(pl.multiple_of(at + o, 128), STRIP)
        return both((dr[:, lanes], dr8[:, lanes]), hi[:, o : o + STRIP], lo[:, o : o + STRIP], TRANSPOSED)

    def by_row(step, hi, lo, o, first):
        i, at, _ = place_of(step)
        lanes = pl.ds(pl.multiple_of(jnp.where(first, LANES, at) + o, 128), STRIP)
        row_acc[:, lanes] += joined(*both((dc[i], dc8[i]), hi[:, o : o + STRIP], lo[:, o : o + STRIP]))

    def half(step, x, x_next, hi, lo, hi_last, lo_last):
        last, following = jnp.maximum(step - 1, 0), jnp.minimum(step + 1, count - 1)
        total = None
        for o in range(0, HALF, STRIP):
            distances(following, x_next, o)
            part = by_col(last, hi_last, lo_last, o)
            total = part if total is None else (total[0] + part[0], total[1] + part[1])
            by_row(last, hi_last, lo_last, o, step == 0)
            got = weights(x[:, o : o + STRIP])
            hi[:, o : o + STRIP], lo[:, o : o + STRIP] = got
        col_acc[jnp.where(step == 0, spare, place_of(last)[0])] += joined(*total)

    for o in range(0, HALF, STRIP):
        distances(0, xa, o)
    early()

    @pl.loop(0, count // 2)
    def _(pair):
        half(2 * pair, xa, xb, ha, la, hb, lb)
        half(2 * pair + 1, xb, xa, hb, lb, ha, la)

    late()
    total = None
    for o in range(0, HALF, STRIP):
        part = by_col(count - 1, hb, lb, o)
        total = part if total is None else (total[0] + part[0], total[1] + part[1])
        by_row(count - 1, hb, lb, o, False)
    col_acc[place_of(count - 1)[0]] += joined(*total)


def stages():
    block = (WIDTH, HALF)
    return [pltpu.VMEM(block, jnp.float32)] * 2 + [pltpu.VMEM(block, jnp.bfloat16)] * 2 + [pltpu.VMEM(block, FINE)] * 2


def folded(x):
    return x[:OBJ] + x[OBJ : 2 * OBJ]


def pack_kernel(points, direction, residual, solution, outscale, noise, out, own, kept):
    wide = direction[...]
    high, low = parts(wide, 2)
    tail = jnp.concatenate([high, low, jnp.zeros((8, WIDTH), jnp.float32)], axis=0)
    tail = tail.astype(jnp.bfloat16)
    own[0, :IN, :] = points[...]
    own[0, IN:, :] = tail
    for i in range(BLOCKS):
        out[i, :IN, :] = points[...]
        out[i, IN:, :] = tail
    kept[0] = wide
    kept[1] = residual[...]
    kept[2] = solution[...]
    for o in range(OBJ):
        kept[3, o : o + 1, :] = jnp.full((1, WIDTH), 3.0 * outscale[o], jnp.float32)
        kept[4, o : o + 1, :] = jnp.full((1, WIDTH), noise[o], jnp.float32)


def near_kernel(place, r0, r1, r2, r3, cols, ax, dr, dr8, row_out, col_near, row_acc, rows, bt, dc, dc8, col_acc, *work):
    y, core, z = place[0], place[1], place[3]
    h = 2 * y + core
    for k, ref in enumerate((r0, r1, r2, r3)):
        rows[2 * k] = ref[0]
        rows[2 * k + 1] = ref[1]
    for i in range(BLOCKS):
        there = lax.rem(h + i, BLOCKS)
        away = lax.rem(y - there // 2 + 4, 4)
        other = jnp.where(lax.rem(there, 2) == core, 0, 1)
        block = rows[2 * away + other]
        lanes = pl.ds(i * WIDTH, WIDTH)
        ax[:, lanes] = row_features(block[:IN])
        tail = block[IN:]
        tail8 = fine(tail)
        dr[:, lanes], dr8[:, lanes] = tail, tail8
        if i < BLOCKS // 2:
            lanes = pl.ds(LANES + i * WIDTH, WIDTH)
            dr[:, lanes] = jnp.zeros_like(tail) if i == 0 else tail
            dr8[:, lanes] = jnp.zeros_like(tail8) if i == 0 else tail8
    row_acc[...] = jnp.zeros_like(row_acc)
    col_acc[...] = jnp.zeros_like(col_acc)

    def features(i):
        block = cols[lax.rem(z + i, BLOCKS)]
        bt[i] = col_features(block[:IN])
        dc[i], dc8[i] = block[IN:], fine(block[IN:])

    features(1)
    tie = jnp.where(z < BLOCKS // 2, 0, WIDTH)

    def place_of(s):
        i = jnp.where(s < 6, 1 + s // 2, jnp.where(s == 6, 4, 0))
        at = jnp.where(s < 6, lax.rem(s, 2) * HALF, jnp.where(s == 6, tie, 0))
        return i, at, jnp.where(s == 7, LANES, at)

    def others():
        for i in (0, 2, 3, 4):
            features(i)

    lanes, found = pl.ds(HALF, WIDTH), []

    def fourth():
        found.extend(weights(dot(bt[0], ax[:, lanes])))

    pipeline(8, 5, place_of, bt, ax, dr, dr8, dc, dc8, row_acc, col_acc, work, others, fourth)
    hi, lo = found
    row_acc[:, lanes] += joined(*both((dc[0], dc8[0]), hi, lo))
    row_out[...] = row_acc[:, :LANES]
    for i in range(BLOCKS):
        got = folded(col_acc[i]) if i < 5 else jnp.zeros((OBJ, WIDTH), jnp.float32)
        col_near[lax.rem(z + i, BLOCKS)] = got


def far_kernel(place, ax, dr, dr8, row_in, cols1, cols2, row_out, col1, col2, row_acc, bt, dc, dc8, col_acc, *work):
    y, core, x, z = place[0], place[1], place[2], place[3]
    h = 2 * y + core
    row_acc[:, :LANES] = row_in[...]
    col_acc[...] = jnp.zeros_like(col_acc)
    first = z + jnp.where(x < 2, 0, 1)

    def features(i):
        block = cols1[i] if i < BLOCKS else cols2[lax.rem(first + i, BLOCKS)]
        bt[i] = col_features(block[:IN])
        dc[i], dc8[i] = block[IN:], fine(block[IN:])

    def others():
        for i in range(1, 12):
            features(i)

    features(0)

    def place_of(s):
        at = lax.rem(s, 2) * HALF
        return s // 2, at, at

    pipeline(24, 12, place_of, bt, ax, dr, dr8, dc, dc8, row_acc, col_acc, work, others)
    for i in range(BLOCKS):
        row_out[lax.rem(h + i, BLOCKS)] = folded(row_acc[:, pl.ds(i * WIDTH, WIDTH)])
        col1[i] = folded(col_acc[i])
        got = folded(col_acc[BLOCKS + i]) if i < 4 else jnp.zeros((OBJ, WIDTH), jnp.float32)
        col2[lax.rem(first + i, BLOCKS)] = got


def join_kernel(near, one, two, out):
    out[...] = near[...] + one[...] + two[...]


def image_kernel(by_rows, by_cols, kept, image, sums):
    total = jnp.zeros((OBJ, WIDTH), jnp.float32)
    for i in range(BLOCKS):
        total = total + by_rows[i] + by_cols[i]
    d, r = kept[0], kept[1]
    got = kept[3] * total + kept[4] * d
    image[...] = got
    products = jnp.concatenate([r * r, d * got, r * got, got * got], axis=0)
    column = jnp.sum(products, axis=1, keepdims=True)
    shape = (4 * OBJ, 128)
    diagonal = lax.broadcasted_iota(jnp.int32, shape, 0) == lax.broadcasted_iota(jnp.int32, shape, 1)
    row = jnp.sum(jnp.where(diagonal, column, 0.0), axis=0, keepdims=True)
    sums[...] = jnp.broadcast_to(row, sums.shape)


def update_kernel(sums, kept, image, solution_new, residual_new, direction_new):
    total = jnp.sum(sums[...], axis=0, keepdims=True)
    lane = lax.broadcasted_iota(jnp.int32, (OBJ, 128), 1) - lax.broadcasted_iota(jnp.int32, (OBJ, 128), 0)

    def kind(k):
        return jnp.sum(jnp.where(lane == k * OBJ, total, 0.0), axis=1, keepdims=True)

    norm_old, curvature, cross, square = kind(0), kind(1), kind(2), kind(3)
    step_len = norm_old / curvature
    norm_new = jnp.maximum(norm_old - 2.0 * step_len * cross + step_len * step_len * square, 0.0)
    ratio_new = norm_new / (norm_old + 1e-06)
    d = kept[0]
    solution_new[...] = kept[2] + step_len * d
    moved = kept[1] - step_len * image[...]
    residual_new[...] = moved
    direction_new[...] = moved + ratio_new * d


def f32(*shape):
    return jax.ShapeDtypeStruct(shape, jnp.float32)


def bf16(*shape):
    return jax.ShapeDtypeStruct(shape, jnp.bfloat16)


def exchanged(x, axis):
    return lax.all_to_all(x, axis, 0, 0)


def from_ahead(x, axis, by):
    length = lax.axis_size(axis)
    return lax.ppermute(x, axis, [(i, (i - by) % length) for i in range(length)])


def shards(points, solution, residual, direction, outscale, noise_var):
    devices = math.prod(SIZES)
    place = jnp.stack([lax.axis_index(a) for a in ("y", "core", "x", "z")]).astype(jnp.int32)
    packed, own, kept = pl.pallas_call(
        pack_kernel,
        in_specs=[VMEM] * 4 + [SMEM] * 2,
        out_specs=[VMEM] * 3,
        out_shape=[bf16(BLOCKS, PACK, WIDTH), bf16(1, PACK, WIDTH), f32(5, OBJ, WIDTH)],
    )(points, direction, residual, solution, outscale, noise_var)
    pair = jnp.concatenate([own, from_ahead(own, "core", 1)], axis=0)
    rows = [pair] + [from_ahead(pair, "y", -k) for k in (1, 2, 3)]
    cols = exchanged(packed, "z")
    cols2, cols1 = from_ahead(cols, "x", 2), from_ahead(cols, "x", 1)
    ax, dr, dr8, row_acc, col_near = pl.pallas_call(
        near_kernel,
        in_specs=[SMEM] + [VMEM] * 5,
        out_specs=[VMEM] * 5,
        out_shape=[
            bf16(DEPTH, LANES),
            bf16(16, LANES + HALF),
            jax.ShapeDtypeStruct((16, LANES + HALF), FINE),
            f32(2 * OBJ, LANES),
            f32(BLOCKS, OBJ, WIDTH),
        ],
        scratch_shapes=[
            pltpu.VMEM((2 * OBJ, LANES + HALF), jnp.float32),
            pltpu.VMEM((BLOCKS, PACK, WIDTH), jnp.bfloat16),
            pltpu.VMEM((5, WIDTH, DEPTH), jnp.bfloat16),
            pltpu.VMEM((5, 16, WIDTH), jnp.bfloat16),
            pltpu.VMEM((5, 16, WIDTH), FINE),
            pltpu.VMEM((6, 2 * OBJ, WIDTH), jnp.float32),
        ]
        + stages(),
        compiler_params=params(),
        cost_estimate=pl.CostEstimate(flops=8 * 10**9, bytes_accessed=10**6, transcendentals=10**7),
    )(place, *rows, cols)
    by_rows, col1, col2 = pl.pallas_call(
        far_kernel,
        in_specs=[SMEM] + [VMEM] * 6,
        out_specs=[VMEM] * 3,
        out_shape=[f32(BLOCKS, OBJ, WIDTH)] * 3,
        scratch_shapes=[
            pltpu.VMEM((2 * OBJ, LANES + HALF), jnp.float32),
            pltpu.VMEM((12, WIDTH, DEPTH), jnp.bfloat16),
            pltpu.VMEM((12, 16, WIDTH), jnp.bfloat16),
            pltpu.VMEM((12, 16, WIDTH), FINE),
            pltpu.VMEM((13, 2 * OBJ, WIDTH), jnp.float32),
        ]
        + stages(),
        compiler_params=params(),
        cost_estimate=pl.CostEstimate(flops=24 * 10**9, bytes_accessed=10**6, transcendentals=10**7),
    )(place, ax, dr, dr8, row_acc, cols1, cols2)
    col2, col1 = from_ahead(col2, "x", -2), from_ahead(col1, "x", -1)
    by_rows = exchanged(by_rows, GROUP)
    by_cols = pl.pallas_call(
        join_kernel,
        in_specs=[VMEM] * 3,
        out_specs=VMEM,
        out_shape=f32(BLOCKS, OBJ, WIDTH),
        compiler_params=params(4),
    )(col_near, col1, col2)
    by_cols = exchanged(by_cols, "z")
    image, sums = pl.pallas_call(
        image_kernel,
        in_specs=[VMEM] * 3,
        out_specs=[VMEM] * 2,
        out_shape=[f32(OBJ, WIDTH), f32(devices, 128)],
        compiler_params=params(4),
    )(by_rows, by_cols, kept)
    sums = exchanged(sums.reshape(devices, 1, 128), AXES).reshape(devices, 128)
    return pl.pallas_call(
        update_kernel,
        in_specs=[VMEM] * 3,
        out_specs=[VMEM] * 3,
        out_shape=[f32(OBJ, WIDTH)] * 3,
        compiler_params=params(4),
    )(sums, kept, image)


def solution(mesh):
    own = Mesh(mesh.devices.reshape(SIZES), AXES)
    split = P(None, AXES)
    return jax.shard_map(
        shards,
        mesh=own,
        in_specs=(split, split, split, split, P(), P()),
        out_specs=(split, split, split),
        check_vma=False,
    )
```
